256 devices in a mesh: grp: 2 (over core), vocab: 32 (over z, y), seq: 4 (over x).
Axes of the slice: x: 4, y: 4, z: 8, core: 2. Of those that a mesh axis runs over, the one named last changes fastest.
Arguments:
- hidden_states: bfloat16 [2, 512, 4096], P('grp', 'seq'), may hold values from -6 to 6
- output_head_weights: bfloat16 [2, 4096, 114688], P('grp', None, ('vocab', 'seq')), may hold values from -0.9375 to 0.9375
- norm_gains: float32 [2, 4096], replicated, may hold values from 0.25 to 1.75
- label_ids: int32 [512], P('seq'), may hold values from 0 to 114687
Outputs:
- token_loss: float32 [512], P('seq')
- head_grad: bfloat16 [4096, 114688], P('grp', ('vocab', 'seq'))
- hidden_grad: bfloat16 [4096, 512], P(('grp', 'vocab', 'seq'))
- gain_grad: float32 [4096], P(('grp', 'vocab', 'seq'))
The draws below stay inside these ranges and needn't reach their ends.
All inputs are finite; a program needn't handle non-finite values.
Results may differ from the reference program's by a relative error of at most 0.0091.
Values may be sent and summed in bfloat16 or wider, within the bound.
A program may use at most 128 MiB of HBM per device.

```python
import math
import jax
import jax.numpy as jnp
import numpy as np
from jax import lax

D = 4096
TOKENS = 512
VOCAB_ENTRIES = 114688


def anchors(key):
    magnitude = jax.random.uniform(jax.random.fold_in(key, 101), (8, D), jnp.float32, 1.5, 2.5)
    signs = jnp.where(jax.random.bernoulli(jax.random.fold_in(key, 104), 0.5, (8, D)), 1.0, -1.0)
    direction = magnitude * signs
    anchor_rows = jax.random.randint(jax.random.fold_in(key, 102), (8,), 0, TOKENS)
    anchor_cols = jax.random.randint(jax.random.fold_in(key, 103), (8,), 0, VOCAB_ENTRIES)
    return (direction, anchor_rows, anchor_cols)


def draw_hidden_states(key, part):
    direction, anchor_rows, anchor_cols = anchors(key)
    key = jax.random.fold_in(key, 1)
    values = jnp.clip(jax.random.normal(key, (2, TOKENS, D), jnp.float32), -6.0, 6.0)
    values = values.at[:, anchor_rows, :].set(direction[None, :, :])
    return values.astype(jnp.bfloat16)


def draw_output_head_weights(key, part):
    direction, anchor_rows, anchor_cols = anchors(key)
    key = jax.random.fold_in(key, 2)
    key_scale, key_noise = jax.random.split(key)
    spread = jnp.exp(jax.random.uniform(key_scale, (2, 1, VOCAB_ENTRIES), jnp.float32, 0.0, math.log(10.0)))
    values = jnp.clip(jax.random.normal(key_noise, (2, D, VOCAB_ENTRIES), jnp.float32), -6.0, 6.0) * spread / math.sqrt(D)
    base = 120.0
    strength = (base + 30.0 * jnp.arange(8, dtype=jnp.float32)) / math.sqrt(D)
    leading = direction.T * strength[None, :] / math.sqrt(D)
    second = direction.T * (strength[None, :] - 2.0 / math.sqrt(D)) / math.sqrt(D)
    values = values.at[:, :, anchor_cols].set(leading[None, :, :])
    values = values.at[:, :, (anchor_cols + 1) % VOCAB_ENTRIES].set(second[None, :, :])
    return values.astype(jnp.bfloat16)


def with_ends(entries, key, smallest, largest):
    index_at = [jax.random.randint(jax.random.fold_in(key, axis), (), 0, length) for axis, length in enumerate(entries.shape)]
    widest = entries.shape.index(max(entries.shape))
    beside = index_at[:widest] + [(index_at[widest] + 1) % entries.shape[widest]] + index_at[widest + 1:]
    return entries.at[tuple(index_at)].set(smallest).at[tuple(beside)].set(largest)


def wide_ids(stream_key, shape, number_of, lean):
    portions = [min(1 << octave, number_of + 1 - (1 << octave)) * (1 << 20) // math.isqrt((1 << octave) ** lean) + 1 for octave in range((number_of + 1).bit_length()) if 1 << octave <= number_of]
    scale = 1 + sum(portions) // (1 << 30)
    table = np.cumsum(np.array([max(1, weight // scale) for weight in portions]))
    lot = jax.random.randint(jax.random.fold_in(stream_key, 1), shape, 0, int(table[len(portions) - 1]))
    start = jnp.left_shift(1, jnp.searchsorted(jnp.asarray(table, jnp.int32), lot, side="right").astype(jnp.int32))
    rank = start - 1 + jax.random.randint(jax.random.fold_in(stream_key, 4), shape, 0, 1 << 30) % jnp.minimum(start, number_of + 1 - start)
    return jax.random.permutation(jax.random.fold_in(stream_key, 2), number_of)[rank].astype(jnp.int32)


def setup_inputs(seed: int = 0) -> dict:
    key_of = jax.random.split(jax.random.key(seed), 5)
    return {
        "hidden_states": draw_hidden_states(jax.random.fold_in(key_of[4], 71), 0),
        "output_head_weights": draw_output_head_weights(jax.random.fold_in(key_of[4], 71), 0),
        "norm_gains": jnp.clip(1.0 + 0.15 * jax.random.normal(key_of[2], (2, D), jnp.float32), 0.25, 1.75),
        "label_ids": with_ends(wide_ids(key_of[3], (TOKENS,), VOCAB_ENTRIES, 2), jax.random.fold_in(key_of[3], 3), 0, VOCAB_ENTRIES - 1).astype(jnp.int32),
    }


SOFTEN_TEMP = 2.0
LABEL_WEIGHT = 0.5
EPSILON = 1e-06

def normalize(states, gain):
    values = states.astype(jnp.float32)
    inverse = lax.rsqrt(lax.optimization_barrier(jnp.mean(values * values, axis=-1, keepdims=True)) + EPSILON)
    unit_vals = values * inverse
    return (unit_vals, inverse, (unit_vals * gain).astype(jnp.bfloat16))

def reference(hidden_states, output_head_weights, norm_gains, label_ids):
    teacher_unit, teacher_inverse, teacher_norm_applied = normalize(hidden_states[0], norm_gains[0])
    student_unit, student_inverse, student_norm_applied = normalize(hidden_states[1], norm_gains[1])
    teacher_scaled_logits = jnp.dot(teacher_norm_applied, output_head_weights[0], preferred_element_type=jnp.float32) / SOFTEN_TEMP
    student_scaled_logits = jnp.dot(student_norm_applied, output_head_weights[1], preferred_element_type=jnp.float32) / SOFTEN_TEMP
    teacher_lse = jax.nn.logsumexp(teacher_scaled_logits, axis=1)
    student_lse = jax.nn.logsumexp(student_scaled_logits, axis=1)
    teacher_prob = jnp.exp(teacher_scaled_logits - teacher_lse[:, None])
    student_prob = jnp.exp(student_scaled_logits - student_lse[:, None])
    columns = jnp.arange(VOCAB_ENTRIES, dtype=jnp.int32)
    target = (columns[None, :] == label_ids[:, None]).astype(jnp.float32)
    picked = lax.optimization_barrier(jnp.sum(target * student_scaled_logits, axis=1))
    divergence = lax.optimization_barrier(jnp.sum(teacher_prob * (teacher_scaled_logits - student_scaled_logits), axis=1)) - teacher_lse + student_lse
    token_loss = divergence + LABEL_WEIGHT * (student_lse - picked)
    scale_factor = VOCAB_ENTRIES / 16.0 / SOFTEN_TEMP
    logit_grad = (scale_factor * ((1.0 + LABEL_WEIGHT) * student_prob - teacher_prob - LABEL_WEIGHT * target)).astype(jnp.bfloat16)
    head_grad = lax.dot_general(student_norm_applied, logit_grad, (((0,), (0,)), ((), ())), preferred_element_type=jnp.float32).astype(jnp.bfloat16)
    normed_grad = lax.dot_general(logit_grad, output_head_weights[1], (((1,), (1,)), ((), ())), preferred_element_type=jnp.float32)
    gain_grad = lax.optimization_barrier(jnp.sum(normed_grad * student_unit, axis=0))
    unit_grad = normed_grad * norm_gains[1]
    row_mean = lax.optimization_barrier(jnp.mean(unit_grad * student_unit, axis=1, keepdims=True))
    hidden_grad = (student_inverse * (unit_grad - student_unit * row_mean)).T.astype(jnp.bfloat16)
    return (token_loss, head_grad, hidden_grad, gain_grad)
```

```python
import jax
import jax.numpy as jnp
from jax import lax
from jax.experimental import pallas as pl
from jax.experimental.pallas import tpu as pltpu
from jax.sharding import PartitionSpec as P

SOFTEN_TEMP = 2.0
LABEL_WEIGHT = 0.5
EPSILON = 1e-06
MESH = pl.DeviceIdType.MESH
F32, BF16 = jnp.float32, jnp.bfloat16
NX, NY, NZ = 4, 4, 8
SUB = 384
Z_BASE = NY * SUB
X_BASE = 2 * NY * SUB
ROWS = 32
PEERS = [(0, 0, d) for d in (1, 2, 3)] + [(0, d, 0) for d in (1, 2, 3)] + [(d, 0, 0) for d in range(1, 8)]


def each(count, body):
    def step(i, carry):
        body(i)
        return carry

    lax.fori_loop(0, count, step, 0)


def kernel(
    hs, w_hbm, gains_hbm, label_hbm,
    loss_out, head_out, hidden_out, gain_out,
    xg, nrm, w, w1h, n1h, n1t, z, zp, e0s, e1s, z1s, lg,
    info, info1, invb, labb, gains, label, xblk, ut,
    statc, st_send, st_recv, lossrt, colb,
    ng, r1, s2, r2, s3, r3, rt_s, rt_r1, rt_r2, rt_r3, fin, hg,
    loc, xs_s, xs_r, ys_s, ys_r, zs_s, zs_r, in_s, in_r, pr_s, pr_r,
    sa_s, sa_r, sz_s, sz_r, ab_s, ab_r, cz_s, cz_r, hg_s,
):
    g = lax.axis_index("grp")
    v = lax.axis_index("vocab")
    s = lax.axis_index("seq")
    zc = lax.div(v, NY)
    yc = lax.rem(v, NY)
    other = 1 - g
    is_teacher = g == 0

    def device(dz, dy, dx):
        return {
            "grp": g,
            "vocab": lax.rem(zc + dz, NZ) * NY + lax.rem(yc + dy, NY),
            "seq": lax.rem(s + dx, NX),
        }

    partner = {"grp": other, "vocab": v, "seq": s}

    def remote(src, dst, ssem, rsem, to):
        return pltpu.make_async_remote_copy(
            src_ref=src, dst_ref=dst, send_sem=ssem, recv_sem=rsem, device_id=to, device_id_type=MESH
        )

    load_x = pltpu.make_async_copy(hs.at[0], xg.at[s], loc.at[0])
    load_g = pltpu.make_async_copy(gains_hbm, gains, loc.at[1])
    load_l = pltpu.make_async_copy(label_hbm, label, loc.at[2])
    load_w = pltpu.make_async_copy(w_hbm.at[0], w, loc.at[3])
    load_x.start()
    load_g.start()
    load_l.start()
    load_w.start()

    barrier = pltpu.get_barrier_semaphore()
    for dz, dy, dx in PEERS:
        pl.semaphore_signal(barrier, inc=1, device_id=device(dz, dy, dx), device_id_type=MESH)
    pl.semaphore_signal(barrier, inc=1, device_id=partner, device_id_type=MESH)
    pl.semaphore_wait(barrier, len(PEERS) + 1)

    zf = lax.div(zc, 2)
    zh = lax.rem(zc, 2)

    def y_cols(y):
        return pl.ds(pl.multiple_of(y * SUB, 128), SUB)

    def z_cols(f):
        return pl.ds(pl.multiple_of(Z_BASE + f * SUB, 128), SUB)

    x_cols = pl.ds(X_BASE, 4096 - X_BASE)

    def z_rows(h):
        return pl.ds(pl.multiple_of(h * 64, 64), 64)

    def x_copy(kind, d, to):
        if kind == 0:
            rows, cols = pl.ds(0, 128), y_cols(yc)
        elif kind == 1:
            rows, cols = z_rows(zh), z_cols(zf)
        else:
            rows, cols = pl.ds(0, 128), x_cols
        at = s if to else lax.rem(s + NX - d, NX)
        dst = xg.at[at, rows, cols]
        return remote(
            hs.at[0, rows, cols] if to else dst, dst, xs_s.at[kind, d - 1], xs_r.at[kind, d - 1], device(0, 0, d)
        )

    for kind in range(3):
        each(3, lambda i, kind=kind: x_copy(kind, i + 1, True).start())

    half_w = pl.ds(0, 2048)

    def w_copy():
        return remote(w_hbm.at[0, half_w, :], w1h, pr_s.at[0], pr_r.at[0], partner)

    load_w1 = pltpu.make_async_copy(w_hbm.at[0, pl.ds(2048, 2048), :], w1h, loc.at[4])

    @pl.when(g == 1)
    def _():
        w_copy().start()
        load_w1.start()

    load_x.wait()
    load_g.wait()
    load_l.wait()
    total = jnp.zeros((128, 128), F32)
    for b in range(32):
        part = xg[s, :, pl.ds(b * 128, 128)].astype(F32)
        total += part * part
    mean = jnp.sum(total, axis=1, keepdims=True) * (1.0 / 4096)
    inverse = lax.rsqrt(mean + EPSILON)
    inverse_rows = jnp.transpose(jnp.broadcast_to(inverse, (128, 128)))[0:8]
    sub8 = lax.broadcasted_iota(jnp.int32, (8, 128), 0)
    label_rows = jnp.broadcast_to(label[...].astype(F32), (8, 128))
    info[s] = jnp.where(sub8 == 1, label_rows, inverse_rows)

    def info_copy(d, to):
        at = s if to else lax.rem(s + NX - d, NX)
        return remote(info.at[at], info.at[at], in_s.at[d - 1], in_r.at[d - 1], device(0, 0, d))

    each(3, lambda i: info_copy(i + 1, True).start())

    def y_copy(dy, d, to):
        shard = lax.rem(s + NX - d, NX)
        y = yc if to else lax.rem(yc + NY - dy, NY)
        ref = xg.at[shard, :, y_cols(y)]
        return remote(ref, ref, ys_s.at[dy - 1, d - 1], ys_r.at[dy - 1, d - 1], device(0, dy, 0))

    def z_copy(dz, d, to):
        shard = lax.rem(s + NX - d, NX)
        at = zc if to else lax.rem(zc + NZ - dz, NZ)
        ref = xg.at[shard, z_rows(lax.rem(at, 2)), z_cols(lax.div(at, 2))]
        return remote(ref, ref, zs_s.at[dz - 1, d - 1], zs_r.at[dz - 1, d - 1], device(dz, 0, 0))

    def forward_y(i):
        x_copy(0, i + 1, False).wait_recv()
        each(3, lambda j: y_copy(j + 1, i + 1, True).start())

    def forward_z(i):
        x_copy(1, i + 1, False).wait_recv()
        each(7, lambda j: z_copy(j + 1, i + 1, True).start())

    each(3, forward_y)
    each(3, forward_z)

    each(3, lambda i: info_copy(i + 1, False).wait_recv())
    tall = jnp.transpose(jnp.concatenate([info[i] for i in range(4)] + [jnp.zeros((96, 128), F32)], axis=0))
    for i in range(4):
        invb[i] = jnp.broadcast_to(tall[:, 8 * i : 8 * i + 1], (128, 128))
        labb[pl.ds(128 * i, 128), :] = jnp.broadcast_to(tall[:, 8 * i + 1 : 8 * i + 2], (128, 128))
    load_w.wait()

    def accumulate(f0, width, first=False):
        for b in range(width // 128):
            cols = pl.ds(pl.multiple_of(f0 + b * 128, 128), 128)
            gain = jnp.where(is_teacher, gains[0:1, cols], gains[1:2, cols])
            for i in range(4):
                unit = xg[i, :, cols].astype(F32) * invb[i]
                nrm[pl.ds(i * 128, 128), cols] = (unit * gain).astype(BF16)
        cols = pl.ds(pl.multiple_of(f0, 128), width)
        product = jnp.dot(nrm[:, cols], w[cols, :], preferred_element_type=F32)
        if first:
            z[...] = product
        else:
            z[...] += product

    accumulate(yc * SUB, SUB, first=True)

    def take_y(i):
        each(3, lambda j: y_copy(i + 1, j + 1, False).wait_recv())
        accumulate(lax.rem(yc + NY - (i + 1), NY) * SUB, SUB)

    each(3, take_y)

    each(3, lambda i: x_copy(2, i + 1, False).wait_recv())
    accumulate(X_BASE, 512)
    accumulate(X_BASE + 512, 512)

    def take_z(dz):
        each(3, lambda j: z_copy(dz, j + 1, False).wait_recv())

    each(7, lambda j: take_z(j + 1))
    each(4, lambda i: accumulate(Z_BASE + i * SUB, SUB))

    own = pl.ds(pl.multiple_of(g * 256, 256), 256)
    theirs = pl.ds(pl.multiple_of(other * 256, 256), 256)
    z_trade = remote(z.at[theirs, :], zp, pr_s.at[1], pr_r.at[1], partner)
    z_trade.start()

    vs = v * NX + s
    teacher_block = lax.div(vs, 8)
    block = g * 16 + teacher_block

    def block_cols(b):
        return pl.ds(pl.multiple_of(b * 128, 128), 128)

    xblk_copy = remote(xg.at[:, :, block_cols(teacher_block)], xblk, pr_s.at[2], pr_r.at[2], partner)
    info_pair = remote(info, info1, pr_s.at[3], pr_r.at[3], partner)
    n1_copy = remote(nrm.at[:, half_w], n1h, pr_s.at[4], pr_r.at[4], partner)
    own_block = pltpu.make_async_copy(xg.at[:, :, block_cols(block)], xblk, loc.at[5])
    own_info = pltpu.make_async_copy(info, info1, loc.at[6])
    own_n1 = pltpu.make_async_copy(nrm.at[:, pl.ds(2048, 2048)], n1h, loc.at[7])

    @pl.when(g == 1)
    def _():
        xblk_copy.start()
        info_pair.start()
        n1_copy.start()
        own_block.start()
        own_info.start()
        own_n1.start()

    z_trade.wait_recv()

    lane = lax.broadcasted_iota(jnp.int32, (ROWS, 128), 1)
    column = lax.broadcasted_iota(jnp.int32, (ROWS, 896), 1)

    def labels_at(r):
        rows = pl.ds(pl.multiple_of(g * 256 + r * ROWS, ROWS), ROWS)
        return labb[rows, 0:1].astype(jnp.int32) - vs * 896

    def totals(r):
        rows = pl.ds(pl.multiple_of(r * ROWS, ROWS), ROWS)
        mine = z[pl.ds(pl.multiple_of(g * 256 + r * ROWS, ROWS), ROWS), :] * (1.0 / SOFTEN_TEMP)
        given = zp[rows, :] * (1.0 / SOFTEN_TEMP)
        z0 = jnp.where(is_teacher, mine, given)
        z1 = jnp.where(is_teacher, given, mine)
        m0 = jnp.max(z0, axis=1, keepdims=True)
        m1 = jnp.max(z1, axis=1, keepdims=True)
        e0 = jnp.exp(z0 - m0)
        e1 = jnp.exp(z1 - m1)
        e0s[rows, :] = e0
        e1s[rows, :] = e1
        z1s[rows, :] = z1
        t0 = jnp.sum(e0, axis=1, keepdims=True)
        t1 = jnp.sum(e1, axis=1, keepdims=True)
        cross = jnp.sum(e0 * (z0 - z1), axis=1, keepdims=True)
        picked = jnp.sum(jnp.where(column == labels_at(r), z1, 0.0), axis=1, keepdims=True)
        stats = jnp.zeros((ROWS, 128), F32)
        for i, value in enumerate((m0, t0, cross, m1, t1, picked)):
            stats = jnp.where(lane == i, value, stats)
        statc[rows, :] = stats

    each(256 // ROWS, totals)
    local = jnp.transpose(statc[...])[0:8]
    st_send[0] = local

    def merge(parts):
        m0 = parts[0][0:1]
        m1 = parts[0][3:4]
        for p in parts[1:]:
            m0 = jnp.maximum(m0, p[0:1])
            m1 = jnp.maximum(m1, p[3:4])
        t0 = cross = t1 = picked = jnp.zeros((1, 256), F32)
        for p in parts:
            s0 = jnp.exp(p[0:1] - m0)
            s1 = jnp.exp(p[3:4] - m1)
            t0 += s0 * p[1:2]
            cross += s0 * p[2:3]
            t1 += s1 * p[4:5]
            picked += p[5:6]
        return jnp.concatenate([m0, t0, cross, m1, t1, picked, picked, picked], axis=0)

    def st_copy(axis, d):
        to = device(0, 0, d) if axis == 0 else device(0, d, 0) if axis == 1 else device(d, 0, 0)
        sems = (sz_s.at[d - 1], sz_r.at[d - 1]) if axis == 2 else (sa_s.at[axis, d - 1], sa_r.at[axis, d - 1])
        return remote(st_send.at[axis], st_recv.at[axis * 3 + d - 1], *sems, to)

    merged = local
    for axis, count in ((0, 3), (1, 3), (2, 7)):
        if axis:
            st_send[axis] = merged
        each(count, lambda i, axis=axis: st_copy(axis, i + 1).start())
        each(count, lambda i, axis=axis: st_copy(axis, i + 1).wait_recv())
        merged = merge([merged] + [st_recv[axis * 3 + i] for i in range(count)])

    lse0 = merged[0:1] + jnp.log(merged[1:2])
    lse1 = merged[3:4] + jnp.log(merged[4:5])
    loss = merged[2:3] / merged[1:2] - lse0 + lse1 + LABEL_WEIGHT * (lse1 - merged[5:6])
    scale = 128 * 896 / 16.0 / SOFTEN_TEMP
    a0 = scale * jnp.exp(local[0:1] - lse0)
    a1 = (scale * (1.0 + LABEL_WEIGHT)) * jnp.exp(local[3:4] - lse1)
    colb[...] = jnp.transpose(jnp.concatenate([a0, a1, jnp.zeros((126, 256), F32)], axis=0))

    def gradient(r):
        rows = pl.ds(pl.multiple_of(r * ROWS, ROWS), ROWS)
        cols = colb[rows, :]
        target = jnp.where(column == labels_at(r), scale * LABEL_WEIGHT, 0.0)
        grad = (cols[:, 1:2] * e1s[rows, :] - cols[:, 0:1] * e0s[rows, :] - target).astype(BF16)
        lg[pl.ds(pl.multiple_of(g * 256 + r * ROWS, ROWS), ROWS), :] = grad
        along = jnp.sum(grad.astype(F32) * z1s[rows, :], axis=1, keepdims=True)
        statc[rows, :] = jnp.broadcast_to(along, (ROWS, 128))

    each(256 // ROWS, gradient)
    lg_trade = remote(lg.at[own, :], lg.at[own, :], pr_s.at[5], pr_r.at[5], partner)
    lg_trade.start()
    along_row = jnp.transpose(statc[...])[0:8]
    sub8w = lax.broadcasted_iota(jnp.int32, (8, 256), 0)
    lossrt[g] = jnp.where(sub8w == 0, jnp.broadcast_to(loss, (8, 256)), along_row)
    rt_trade = remote(lossrt.at[g], lossrt.at[g], pr_s.at[6], pr_r.at[6], partner)
    rt_trade.start()

    @pl.when(g == 0)
    def _():
        w_copy().wait_recv()

    @pl.when(g == 1)
    def _():
        load_w1.wait()

    def states_grad(h):
        tokens = lg[pl.ds(pl.multiple_of(h * 256, 256), 256), :]

        def tile(i):
            rows = w1h[pl.ds(pl.multiple_of(i * 512, 512), 512), :]
            product = lax.dot_general(rows, tokens, (((1,), (1,)), ((), ())), preferred_element_type=F32)
            for k in range(2):
                for y in range(NY):
                    for x in range(NX):
                        at = k * 256 + (y * NX + x) * 16
                        a = x + (y - x) * h
                        b = y + (x - y) * h
                        ng[h, a, b, 2 * i + k] = product[at : at + 16].astype(BF16)

        each(4, tile)

    def first(h):
        return s + (yc - s) * h

    def second(h):
        return yc + (s - yc) * h

    def a_copy(h, d):
        to = device(0, d * h, d * (1 - h))
        return remote(ng.at[h, lax.rem(first(h) + d, 4)], r1.at[h, d - 1], ab_s.at[h, 0, d - 1], ab_r.at[h, 0, d - 1], to)

    def at_copy(h, d):
        to = device(0, d * h, d * (1 - h))
        return remote(lossrt.at[h], rt_r1.at[h, d - 1], ab_s.at[h, 1, d - 1], ab_r.at[h, 1, d - 1], to)

    def b_copy(h, d):
        to = device(0, d * (1 - h), d * h)
        return remote(s2.at[h, lax.rem(second(h) + d, 4)], r2.at[h, d - 1], ab_s.at[h, 2, d - 1], ab_r.at[h, 2, d - 1], to)

    def bt_copy(h, d):
        to = device(0, d * (1 - h), d * h)
        return remote(rt_s.at[h, 0], rt_r2.at[h, d - 1], ab_s.at[h, 3, d - 1], ab_r.at[h, 3, d - 1], to)

    def c_copy(h, d):
        return remote(s3.at[h, lax.rem(zc + d, NZ)], r3.at[h, d - 1], cz_s.at[h, 0, d - 1], cz_r.at[h, 0, d - 1], device(d, 0, 0))

    def ct_copy(h, d):
        return remote(rt_s.at[h, 1], rt_r3.at[h, d - 1], cz_s.at[h, 1, d - 1], cz_r.at[h, 1, d - 1], device(d, 0, 0))

    def start_a(h):
        def go(i):
            a_copy(h, i + 1).start()
            at_copy(h, i + 1).start()

        each(3, go)

    def start_b(h):
        def got(i):
            a_copy(h, i + 1).wait_recv()
            at_copy(h, i + 1).wait_recv()

        each(3, got)
        mine = first(h)

        def add(b):
            for k in range(NZ):
                total = ng[h, mine, b, k].astype(F32)
                for i in range(3):
                    total += r1[h, i, b, k].astype(F32)
                s2[h, b, k] = total.astype(BF16)

        each(4, add)
        rt_s[h, 0] = lossrt[h] + rt_r1[h, 0] + rt_r1[h, 1] + rt_r1[h, 2]

        def go(i):
            b_copy(h, i + 1).start()
            bt_copy(h, i + 1).start()

        each(3, go)

    def start_c(h):
        def got(i):
            b_copy(h, i + 1).wait_recv()
            bt_copy(h, i + 1).wait_recv()

        each(3, got)
        mine = second(h)
        for k in range(NZ):
            total = s2[h, mine, k].astype(F32)
            for i in range(3):
                total += r2[h, i, k].astype(F32)
            s3[h, k] = total.astype(BF16)
        rt_s[h, 1] = rt_s[h, 0] + rt_r2[h, 0] + rt_r2[h, 1] + rt_r2[h, 2]

        def go(i):
            c_copy(h, i + 1).start()
            ct_copy(h, i + 1).start()

        each(7, go)

    def finish(h):
        def got(i):
            c_copy(h, i + 1).wait_recv()
            ct_copy(h, i + 1).wait_recv()

        each(7, got)
        total = s3[h, zc].astype(F32)
        along = rt_s[h, 1]
        for i in range(7):
            total += r3[h, i].astype(F32)
            along += rt_r3[h, i]
        fin[h] = total
        rt_s[h, 2] = along

    states_grad(g)
    start_a(g)
    lg_trade.wait()
    rt_trade.wait()
    states_grad(other)
    start_a(other)

    @pl.when(g == 0)
    def _():
        n1_copy.wait_recv()
        xblk_copy.wait_recv()
        info_pair.wait_recv()

    @pl.when(g == 1)
    def _():
        own_n1.wait()
        own_block.wait()
        own_info.wait()

    def flip(i):
        cols = pl.ds(pl.multiple_of(i * 128, 128), 128)
        n1t[cols, :] = jnp.transpose(n1h[:, cols])

    each(16, flip)

    def head_store(i):
        rows = pl.ds(pl.multiple_of(i * 512, 512), 512)
        return pltpu.make_async_copy(hg.at[rows, :], head_out.at[rows, :], hg_s.at[i])

    def head_tile(i):
        rows = pl.ds(pl.multiple_of(i * 512, 512), 512)
        hg[rows, :] = jnp.dot(n1t[rows, :], lg[...], preferred_element_type=F32).astype(BF16)
        head_store(i).start()

    each(4, head_tile)

    inv_row = jnp.concatenate([info1[i, 0:1] for i in range(4)], axis=1)
    for i in range(4):
        unit = jnp.transpose(xblk[i].astype(F32)) * info1[i, 0:1]
        ut[:, pl.ds(i * 128, 128)] = unit
    gain_col = jnp.transpose(jnp.broadcast_to(gains[1:2, block_cols(block)], (128, 128)))
    statc[pl.ds(0, 128), :] = gain_col

    start_b(g)
    start_b(other)
    start_c(g)
    start_c(other)
    finish(g)
    finish(other)

    mine16 = pl.ds(pl.multiple_of(lax.rem(vs, 8) * 16, 16), 16)
    gain16 = statc[mine16, 0:1]
    gain_total = jnp.zeros((16, 1), F32)
    for h in range(2):
        cols = pl.ds(h * 256, 256)
        unit = ut[mine16, cols]
        grad = fin[h]
        row_mean = rt_s[h, 2][1:2] * (SOFTEN_TEMP / 4096)
        hidden = inv_row[:, h * 256 : h * 256 + 256] * (grad * gain16 - unit * row_mean)
        hidden_out[:, cols] = hidden.astype(BF16)
        gain_total += jnp.sum(grad * unit, axis=1, keepdims=True)
    wide = jnp.concatenate([jnp.broadcast_to(gain_total, (16, 128)), jnp.zeros((112, 128), F32)], axis=0)
    gain_out[...] = jnp.transpose(wide)[0:1]
    loss_out[...] = lossrt[lax.div(s, 2), 0:1, pl.ds(pl.multiple_of(lax.rem(s, 2) * 128, 128), 128)]

    for kind in range(3):
        each(3, lambda i, kind=kind: x_copy(kind, i + 1, True).wait_send())

    def sent_yz(i):
        info_copy(i + 1, True).wait_send()
        each(3, lambda j: y_copy(j + 1, i + 1, True).wait_send())
        each(7, lambda j: z_copy(j + 1, i + 1, True).wait_send())

    each(3, sent_yz)
    z_trade.wait_send()

    @pl.when(g == 1)
    def _():
        w_copy().wait_send()
        xblk_copy.wait_send()
        info_pair.wait_send()
        n1_copy.wait_send()

    for axis, count in ((0, 3), (1, 3), (2, 7)):
        each(count, lambda i, axis=axis: st_copy(axis, i + 1).wait_send())

    def sent_ab(h):
        def one(i):
            a_copy(h, i + 1).wait_send()
            at_copy(h, i + 1).wait_send()
            b_copy(h, i + 1).wait_send()
            bt_copy(h, i + 1).wait_send()

        def two(i):
            c_copy(h, i + 1).wait_send()
            ct_copy(h, i + 1).wait_send()

        each(3, one)
        each(7, two)

    each(2, sent_ab)
    each(4, lambda i: head_store(i).wait())


def per_device(hidden_states, output_head_weights, norm_gains, label_ids):
    dma = pltpu.SemaphoreType.DMA
    vm = pltpu.VMEM
    scratch = [
        vm((4, 128, 4096), BF16),
        vm((512, 4096), BF16),
        vm((4096, 896), BF16),
        vm((2048, 896), BF16),
        vm((512, 2048), BF16),
        vm((2048, 512), BF16),
        vm((512, 896), F32),
        vm((256, 896), F32),
        vm((256, 896), F32),
        vm((256, 896), F32),
        vm((256, 896), F32),
        vm((512, 896), BF16),
        vm((4, 8, 128), F32),
        vm((4, 8, 128), F32),
        vm((4, 128, 128), F32),
        vm((512, 128), F32),
        vm((2, 4096), F32),
        vm((1, 128), jnp.int32),
        vm((4, 128, 128), BF16),
        vm((128, 512), F32),
        vm((256, 128), F32),
        vm((3, 8, 256), F32),
        vm((13, 8, 256), F32),
        vm((2, 8, 256), F32),
        vm((256, 128), F32),
        vm((2, 4, 4, 8, 16, 256), BF16),
        vm((2, 3, 4, 8, 16, 256), BF16),
        vm((2, 4, 8, 16, 256), BF16),
        vm((2, 3, 8, 16, 256), BF16),
        vm((2, 8, 16, 256), BF16),
        vm((2, 7, 16, 256), BF16),
        vm((2, 3, 8, 256), F32),
        vm((2, 3, 8, 256), F32),
        vm((2, 3, 8, 256), F32),
        vm((2, 7, 8, 256), F32),
        vm((2, 16, 256), F32),
        vm((2048, 896), BF16),
        dma((8,)),
        dma((3, 3)), dma((3, 3)),
        dma((3, 3)), dma((3, 3)),
        dma((7, 3)), dma((7, 3)),
        dma((3,)), dma((3,)),
        dma((7,)), dma((7,)),
        dma((2, 3)), dma((2, 3)),
        dma((7,)), dma((7,)),
        dma((2, 4, 3)), dma((2, 4, 3)),
        dma((2, 2, 7)), dma((2, 2, 7)),
        dma((4,)),
    ]
    whole = pl.BlockSpec(memory_space=pl.ANY)
    vmem = pl.BlockSpec(memory_space=pltpu.VMEM)
    loss, head_grad, hidden_grad, gain_grad = pl.pallas_call(
        kernel,
        name="distill",
        out_shape=(
            jax.ShapeDtypeStruct((1, 128), F32),
            jax.ShapeDtypeStruct((2048, 896), BF16),
            jax.ShapeDtypeStruct((16, 512), BF16),
            jax.ShapeDtypeStruct((1, 128), F32),
        ),
        in_specs=[whole] * 4,
        out_specs=(vmem, whole, vmem, vmem),
        scratch_shapes=scratch,
        cost_estimate=pl.CostEstimate(flops=10**10, bytes_accessed=2 * 10**7, transcendentals=10**6),
        compiler_params=pltpu.CompilerParams(
            collective_id=0, has_side_effects=True, vmem_limit_bytes=60 * 2**20
        ),
    )(hidden_states, output_head_weights, norm_gains, label_ids.reshape(1, 128))
    return loss.reshape(128), head_grad, hidden_grad, gain_grad[0, :16]


def solution(mesh):
    placed = (P("grp", "seq", None), P("grp", None, ("vocab", "seq")), P(), P("seq"))
    return jax.shard_map(
        per_device,
        mesh=mesh,
        in_specs=placed,
        out_specs=(
            P("seq"),
            P("grp", ("vocab", "seq")),
            P(("grp", "vocab", "seq"), None),
            P(("grp", "vocab", "seq")),
        ),
        check_vma=False,
    )
```

```python
import jax
import jax.numpy as jnp
from jax import lax
from jax.experimental import pallas as pl
from jax.experimental.pallas import tpu as pltpu
from jax.sharding import PartitionSpec as P

SOFTEN_TEMP = 2.0
LABEL_WEIGHT = 0.5
EPSILON = 1e-06
MESH = pl.DeviceIdType.MESH
F32, BF16 = jnp.float32, jnp.bfloat16
NX, NY, NZ = 4, 4, 8
Y_SUB, Z_SUB = 512, 128
Z_BASE = NY * Y_SUB
X_BASE = Z_BASE + NZ * Z_SUB
ROWS = 32
PEERS = [(0, 0, d) for d in (1, 2, 3)] + [(0, d, 0) for d in (1, 2, 3)] + [(d, 0, 0) for d in range(1, 8)]


def each(count, body):
    def step(i, carry):
        body(i)
        return carry

    lax.fori_loop(0, count, step, 0)


def kernel(
    hs, w_hbm, gains_hbm, label_hbm,
    loss_out, head_out, hidden_out, gain_out,
    xg, nrm, w, w1h, n1h, n1t, z, zp, e0s, e1s, z1s, lg,
    info, info1, invb, labb, gains, label, xblk, ut,
    statc, st_send, st_recv, lossrt, colb,
    ng, q1, q2, r1, s2, r2, s3, r3, rt_s, rt_r1, rt_r2, rt_r3, fin,
    loc, xs_s, xs_r, ys_s, ys_r, zs_s, zs_r, in_s, in_r, pr_s, pr_r,
    sa_s, sa_r, sz_s, sz_r, ab_s, ab_r, cz_s, cz_r,
):
    g = lax.axis_index("grp")
    v = lax.axis_index("vocab")
    s = lax.axis_index("seq")
    zc = lax.div(v, NY)
    yc = lax.rem(v, NY)
    other = 1 - g
    is_teacher = g == 0

    def device(dz, dy, dx):
        return {
            "grp": g,
            "vocab": lax.rem(zc + dz, NZ) * NY + lax.rem(yc + dy, NY),
            "seq": lax.rem(s + dx, NX),
        }

    partner = {"grp": other, "vocab": v, "seq": s}

    def remote(src, dst, ssem, rsem, to):
        return pltpu.make_async_remote_copy(
            src_ref=src, dst_ref=dst, send_sem=ssem, recv_sem=rsem, device_id=to, device_id_type=MESH
        )

    load_x = pltpu.make_async_copy(hs.at[0], xg.at[s], loc.at[0])
    load_g = pltpu.make_async_copy(gains_hbm, gains, loc.at[1])
    load_l = pltpu.make_async_copy(label_hbm, label, loc.at[2])
    load_w = pltpu.make_async_copy(w_hbm.at[0], w, loc.at[3])
    load_x.start()
    load_g.start()
    load_l.start()
    load_w.start()

    barrier = pltpu.get_barrier_semaphore()
    for dz, dy, dx in PEERS:
        pl.semaphore_signal(barrier, inc=1, device_id=device(dz, dy, dx), device_id_type=MESH)
    pl.semaphore_signal(barrier, inc=1, device_id=partner, device_id_type=MESH)
    load_x.wait()
    load_g.wait()
    load_l.wait()
    total = jnp.zeros((128, 128), F32)
    for b in range(32):
        part = xg[s, :, pl.ds(b * 128, 128)].astype(F32)
        total += part * part
    mean = jnp.sum(total, axis=1, keepdims=True) * (1.0 / 4096)
    inverse = lax.rsqrt(mean + EPSILON)
    inverse_rows = jnp.transpose(jnp.broadcast_to(inverse, (128, 128)))[0:8]
    sub8 = lax.broadcasted_iota(jnp.int32, (8, 128), 0)
    label_rows = jnp.broadcast_to(label[...].astype(F32), (8, 128))
    info[s] = jnp.where(sub8 == 1, label_rows, inverse_rows)

    pl.semaphore_wait(barrier, len(PEERS) + 1)

    def y_cols(y):
        return pl.ds(pl.multiple_of(y * Y_SUB, 128), Y_SUB)

    def y_half(y, k):
        return pl.ds(pl.multiple_of(y * Y_SUB + k * (Y_SUB // 2), 128), Y_SUB // 2)

    def z_cols(at):
        return pl.ds(pl.multiple_of(Z_BASE + at * Z_SUB, 128), Z_SUB)

    def x_copy(kind, d, to):
        cols = (y_cols(yc), z_cols(zc), pl.ds(X_BASE, 4096 - X_BASE))[kind]
        at = s if to else lax.rem(s + NX - d, NX)
        dst = xg.at[at, :, cols]
        return remote(
            hs.at[0, :, cols] if to else dst, dst, xs_s.at[kind, d - 1], xs_r.at[kind, d - 1], device(0, 0, d)
        )

    def x_start(kind):
        each(3, lambda i: x_copy(kind, i + 1, True).start())

    def info_copy(d, to):
        at = s if to else lax.rem(s + NX - d, NX)
        return remote(info.at[at], info.at[at], in_s.at[d - 1], in_r.at[d - 1], device(0, 0, d))

    x_start(1)
    x_start(0)
    each(3, lambda i: info_copy(i + 1, True).start())

    half_w = pl.ds(0, 2048)

    def w_copy():
        return remote(w_hbm.at[0, half_w, :], w1h, pr_s.at[0], pr_r.at[0], partner)

    load_w1 = pltpu.make_async_copy(w_hbm.at[0, pl.ds(2048, 2048), :], w1h, loc.at[4])

    @pl.when(g == 1)
    def _():
        w_copy().start()
        load_w1.start()

    def y_copy(k, d, to):
        shard = lax.rem(s + NX - d, NX)
        dy = 1 + 2 * k
        ref = xg.at[shard, :, y_cols(yc if to else lax.rem(yc + NY - dy, NY))]
        return remote(ref, ref, ys_s.at[k, d - 1], ys_r.at[k, d - 1], device(0, dy, 0))

    def y_relay(k, d, to):
        shard = lax.rem(s + NX - d, NX)
        dy = 1 + 2 * k
        ref = xg.at[shard, :, y_half(lax.rem(yc + (NY - dy if to else 2), NY), k)]
        return remote(ref, ref, ys_s.at[2 + k, d - 1], ys_r.at[2 + k, d - 1], device(0, dy, 0))

    def z_copy(dz, d, to):
        shard = lax.rem(s + NX - d, NX)
        ref = xg.at[shard, :, z_cols(zc if to else lax.rem(zc + NZ - dz, NZ))]
        return remote(ref, ref, zs_s.at[dz - 1, d - 1], zs_r.at[dz - 1, d - 1], device(dz, 0, 0))

    def forward_z(i):
        x_copy(1, i + 1, False).wait_recv()
        each(7, lambda j: z_copy(j + 1, i + 1, True).start())

    def forward_y(i):
        x_copy(0, i + 1, False).wait_recv()
        y_copy(0, i + 1, True).start()
        y_copy(1, i + 1, True).start()

    each(3, forward_z)
    each(3, forward_y)
    x_start(2)

    each(3, lambda i: info_copy(i + 1, False).wait_recv())
    tall = jnp.transpose(jnp.concatenate([info[i] for i in range(4)] + [jnp.zeros((96, 128), F32)], axis=0))
    for i in range(4):
        invb[i] = jnp.broadcast_to(tall[:, 8 * i : 8 * i + 1], (128, 128))
        labb[pl.ds(128 * i, 128), :] = jnp.broadcast_to(tall[:, 8 * i + 1 : 8 * i + 2], (128, 128))
    load_w.wait()

    def accumulate(f0, width, first=False):
        for b in range(width // 128):
            cols = pl.ds(pl.multiple_of(f0 + b * 128, 128), 128)
            gain = jnp.where(is_teacher, gains[0:1, cols], gains[1:2, cols])
            for i in range(4):
                unit = xg[i, :, cols].astype(F32) * invb[i]
                nrm[pl.ds(i * 128, 128), cols] = (unit * gain).astype(BF16)
        cols = pl.ds(pl.multiple_of(f0, 128), width)
        product = jnp.dot(nrm[:, cols], w[cols, :], preferred_element_type=F32)
        if first:
            z[...] = product
        else:
            z[...] += product

    accumulate(yc * Y_SUB, Y_SUB, first=True)

    def pass_y(i):
        for k in range(2):
            y_copy(k, i + 1, False).wait_recv()
            y_relay(k, i + 1, True).start()

    each(3, pass_y)

    def add_y(i):
        accumulate(lax.rem(yc + 1 + 2 * i, NY) * Y_SUB, Y_SUB)

    each(2, add_y)

    each(3, lambda i: x_copy(2, i + 1, False).wait_recv())
    accumulate(X_BASE, 512)
    accumulate(X_BASE + 512, 512)

    def take_y(i):
        y_relay(0, i + 1, False).wait_recv()
        y_relay(1, i + 1, False).wait_recv()

    each(3, take_y)
    accumulate(lax.rem(yc + 2, NY) * Y_SUB, Y_SUB)

    def take_z(i):
        each(3, lambda j: z_copy(i + 1, j + 1, False).wait_recv())

    each(7, take_z)
    accumulate(Z_BASE, 512)
    accumulate(Z_BASE + 512, 512)

    own = pl.ds(pl.multiple_of(g * 256, 256), 256)
    theirs = pl.ds(pl.multiple_of(other * 256, 256), 256)
    z_trade = remote(z.at[theirs, :], zp, pr_s.at[1], pr_r.at[1], partner)
    z_trade.start()

    vs = v * NX + s
    teacher_block = lax.div(vs, 8)
    block = g * 16 + teacher_block

    def block_cols(b):
        return pl.ds(pl.multiple_of(b * 128, 128), 128)

    xblk_copy = remote(xg.at[:, :, block_cols(teacher_block)], xblk, pr_s.at[2], pr_r.at[2], partner)
    info_pair = remote(info, info1, pr_s.at[3], pr_r.at[3], partner)
    n1_copy = remote(nrm.at[:, half_w], n1h, pr_s.at[4], pr_r.at[4], partner)
    own_block = pltpu.make_async_copy(xg.at[:, :, block_cols(block)], xblk, loc.at[5])
    own_info = pltpu.make_async_copy(info, info1, loc.at[6])
    own_n1 = pltpu.make_async_copy(nrm.at[:, pl.ds(2048, 2048)], n1h, loc.at[7])

    z_trade.wait()

    @pl.when(g == 1)
    def _():
        xblk_copy.start()
        info_pair.start()
        n1_copy.start()
        own_block.start()
        own_info.start()
        own_n1.start()

    lane = lax.broadcasted_iota(jnp.int32, (ROWS, 128), 1)
    column = lax.broadcasted_iota(jnp.int32, (ROWS, 896), 1)

    def labels_at(r):
        rows = pl.ds(pl.multiple_of(g * 256 + r * ROWS, ROWS), ROWS)
        return labb[rows, 0:1].astype(jnp.int32) - vs * 896

    def totals(r):
        rows = pl.ds(pl.multiple_of(r * ROWS, ROWS), ROWS)
        mine = z[pl.ds(pl.multiple_of(g * 256 + r * ROWS, ROWS), ROWS), :] * (1.0 / SOFTEN_TEMP)
        given = zp[rows, :] * (1.0 / SOFTEN_TEMP)
        z0 = jnp.where(is_teacher, mine, given)
        z1 = jnp.where(is_teacher, given, mine)
        m0 = jnp.max(z0, axis=1, keepdims=True)
        m1 = jnp.max(z1, axis=1, keepdims=True)
        e0 = jnp.exp(z0 - m0)
        e1 = jnp.exp(z1 - m1)
        e0s[rows, :] = e0
        e1s[rows, :] = e1
        z1s[rows, :] = z1
        t0 = jnp.sum(e0, axis=1, keepdims=True)
        t1 = jnp.sum(e1, axis=1, keepdims=True)
        cross = jnp.sum(e0 * (z0 - z1), axis=1, keepdims=True)
        picked = jnp.sum(jnp.where(column == labels_at(r), z1, 0.0), axis=1, keepdims=True)
        stats = jnp.zeros((ROWS, 128), F32)
        for i, value in enumerate((m0, t0, cross, m1, t1, picked)):
            stats = jnp.where(lane == i, value, stats)
        statc[rows, :] = stats

    each(256 // ROWS, totals)
    local = jnp.transpose(statc[...])[0:8]
    st_send[0] = local

    def merge(parts):
        m0 = parts[0][0:1]
        m1 = parts[0][3:4]
        for p in parts[1:]:
            m0 = jnp.maximum(m0, p[0:1])
            m1 = jnp.maximum(m1, p[3:4])
        t0 = cross = t1 = picked = jnp.zeros((1, 256), F32)
        for p in parts:
            s0 = jnp.exp(p[0:1] - m0)
            s1 = jnp.exp(p[3:4] - m1)
            t0 += s0 * p[1:2]
            cross += s0 * p[2:3]
            t1 += s1 * p[4:5]
            picked += p[5:6]
        return jnp.concatenate([m0, t0, cross, m1, t1, picked, picked, picked], axis=0)

    def st_copy(axis, d):
        to = device(0, 0, d) if axis == 0 else device(0, d, 0) if axis == 1 else device(d, 0, 0)
        sems = (sz_s.at[d - 1], sz_r.at[d - 1]) if axis == 2 else (sa_s.at[axis, d - 1], sa_r.at[axis, d - 1])
        return remote(st_send.at[axis], st_recv.at[axis * 3 + d - 1], *sems, to)

    merged = local
    for axis, count in ((0, 3), (1, 3), (2, 7)):
        if axis:
            st_send[axis] = merged
        each(count, lambda i, axis=axis: st_copy(axis, i + 1).start())
        each(count, lambda i, axis=axis: st_copy(axis, i + 1).wait_recv())
        merged = merge([merged] + [st_recv[axis * 3 + i] for i in range(count)])

    lse0 = merged[0:1] + jnp.log(merged[1:2])
    lse1 = merged[3:4] + jnp.log(merged[4:5])
    loss = merged[2:3] / merged[1:2] - lse0 + lse1 + LABEL_WEIGHT * (lse1 - merged[5:6])
    scale = 128 * 896 / 16.0 / SOFTEN_TEMP
    a0 = scale * jnp.exp(local[0:1] - lse0)
    a1 = (scale * (1.0 + LABEL_WEIGHT)) * jnp.exp(local[3:4] - lse1)
    colb[...] = jnp.transpose(jnp.concatenate([a0, a1, jnp.zeros((126, 256), F32)], axis=0))

    def gradient(r):
        rows = pl.ds(pl.multiple_of(r * ROWS, ROWS), ROWS)
        cols = colb[rows, :]
        target = jnp.where(column == labels_at(r), scale * LABEL_WEIGHT, 0.0)
        grad = (cols[:, 1:2] * e1s[rows, :] - cols[:, 0:1] * e0s[rows, :] - target).astype(BF16)
        lg[pl.ds(pl.multiple_of(g * 256 + r * ROWS, ROWS), ROWS), :] = grad
        along = jnp.sum(grad.astype(F32) * z1s[rows, :], axis=1, keepdims=True)
        statc[rows, :] = jnp.broadcast_to(along, (ROWS, 128))

    each(256 // ROWS, gradient)
    lg_trade = remote(lg.at[own, :], lg.at[own, :], pr_s.at[5], pr_r.at[5], partner)
    lg_trade.start()

    @pl.when(g == 0)
    def _():
        w_copy().wait_recv()

    @pl.when(g == 1)
    def _():
        load_w1.wait()

    def states_grad(h):
        tokens = lg[pl.ds(pl.multiple_of(h * 256, 256), 256), :]

        def tile(i):
            rows = w1h[pl.ds(pl.multiple_of(i * 512, 512), 512), :]
            product = lax.dot_general(rows, tokens, (((1,), (1,)), ((), ())), preferred_element_type=F32)
            for k in range(2):
                for y in range(NY):
                    for x in range(NX):
                        at = k * 256 + (y * NX + x) * 16
                        a = x + (y - x) * h
                        b = y + (x - y) * h
                        ng[h, a, b, 2 * i + k] = product[at : at + 16].astype(BF16)

        each(4, tile)

    def first(h):
        return s + (yc - s) * h

    def second(h):
        return yc + (s - yc) * h

    def a_copy(h, k, part):
        d = 1 + 2 * k
        to = device(0, d * h, d * (1 - h))
        blocks = pl.ds(2 * ((k + part) % 2), 2)
        sems = (ab_s.at[h, k, part], ab_r.at[h, k, part])
        if part == 0:
            return remote(ng.at[h, lax.rem(first(h) + 2, 4), blocks], q1.at[h, k], *sems, to)
        src = ng.at[h, lax.rem(first(h) + d, 4), blocks] if part == 1 else q2.at[h, k]
        return remote(src, r1.at[h, k, blocks], *sems, to)

    def at_copy(h, d):
        to = device(0, d * h, d * (1 - h))
        return remote(lossrt.at[h], rt_r1.at[h, d - 1], ab_s.at[h, 2, d - 1], ab_r.at[h, 2, d - 1], to)

    def b_copy(h, d):
        to = device(0, d * (1 - h), d * h)
        return remote(s2.at[h, lax.rem(second(h) + d, 4)], r2.at[h, d - 1], ab_s.at[h, 3, d - 1], ab_r.at[h, 3, d - 1], to)

    def bt_copy(h, d):
        to = device(0, d * (1 - h), d * h)
        return remote(rt_s.at[h, 0], rt_r2.at[h, d - 1], ab_s.at[h, 4, d - 1], ab_r.at[h, 4, d - 1], to)

    def c_copy(h, d):
        return remote(s3.at[h, lax.rem(zc + d, NZ)], r3.at[h, d - 1], cz_s.at[h, 0, d - 1], cz_r.at[h, 0, d - 1], device(d, 0, 0))

    def ct_copy(h, d):
        return remote(rt_s.at[h, 1], rt_r3.at[h, d - 1], cz_s.at[h, 1, d - 1], cz_r.at[h, 1, d - 1], device(d, 0, 0))

    def start_a(h):
        for part in range(2):
            for k in range(2):
                a_copy(h, k, part).start()

    def start_at(h):
        each(3, lambda i: at_copy(h, i + 1).start())

    def pass_a(h):
        for k in range(2):
            a_copy(h, k, 0).wait_recv()
            at = lax.rem(first(h) + 1 + 2 * k, 4)

            def add(i, k=k, at=at):
                for b in range(2):
                    q2[h, k, b, i] = (ng[h, at, 2 * k + b, i].astype(F32) + q1[h, k, b, i].astype(F32)).astype(BF16)

            each(NZ, add)
            a_copy(h, k, 2).start()

    def start_b(h):
        each(3, lambda i: at_copy(h, i + 1).wait_recv())
        for k in range(2):
            a_copy(h, k, 1).wait_recv()
            a_copy(h, k, 2).wait_recv()
        mine = first(h)

        def add(b):
            for k in range(NZ):
                total = ng[h, mine, b, k].astype(F32)
                for i in range(2):
                    total += r1[h, i, b, k].astype(F32)
                s2[h, b, k] = total.astype(BF16)

        each(4, add)
        rt_s[h, 0] = lossrt[h] + rt_r1[h, 0] + rt_r1[h, 1] + rt_r1[h, 2]

        def go(i):
            b_copy(h, i + 1).start()
            bt_copy(h, i + 1).start()

        each(3, go)

    def start_c(h):
        def got(i):
            b_copy(h, i + 1).wait_recv()
            bt_copy(h, i + 1).wait_recv()

        each(3, got)
        mine = second(h)
        for k in range(NZ):
            total = s2[h, mine, k].astype(F32)
            for i in range(3):
                total += r2[h, i, k].astype(F32)
            s3[h, k] = total.astype(BF16)
        rt_s[h, 1] = rt_s[h, 0] + rt_r2[h, 0] + rt_r2[h, 1] + rt_r2[h, 2]

        def go(i):
            c_copy(h, i + 1).start()
            ct_copy(h, i + 1).start()

        each(7, go)

    def finish(h):
        def got(i):
            c_copy(h, i + 1).wait_recv()
            ct_copy(h, i + 1).wait_recv()

        each(7, got)
        total = s3[h, zc].astype(F32)
        along = rt_s[h, 1]
        for i in range(7):
            total += r3[h, i].astype(F32)
            along += rt_r3[h, i]
        fin[h] = total
        rt_s[h, 2] = along

    states_grad(g)
    start_a(g)
    lg_trade.wait_recv()
    states_grad(other)
    start_a(other)

    along_row = jnp.transpose(statc[...])[0:8]
    sub8w = lax.broadcasted_iota(jnp.int32, (8, 256), 0)
    lossrt[g] = jnp.where(sub8w == 0, jnp.broadcast_to(loss, (8, 256)), along_row)
    rt_trade = remote(lossrt.at[g], lossrt.at[g], pr_s.at[6], pr_r.at[6], partner)
    rt_trade.start()

    start_at(g)
    rt_trade.wait()
    lg_trade.wait_send()
    start_at(other)

    @pl.when(g == 0)
    def _():
        n1_copy.wait_recv()
        xblk_copy.wait_recv()
        info_pair.wait_recv()

    @pl.when(g == 1)
    def _():
        own_n1.wait()
        own_block.wait()
        own_info.wait()

    def flip(i):
        cols = pl.ds(pl.multiple_of(i * 128, 128), 128)
        n1t[cols, :] = jnp.transpose(n1h[:, cols])

    each(16, flip)

    pass_a(g)

    def head_tile(i):
        rows = pl.ds(pl.multiple_of(i * 512, 512), 512)
        head_out[rows, :] = jnp.dot(n1t[rows, :], lg[...], preferred_element_type=F32).astype(BF16)

    each(2, head_tile)
    pass_a(other)
    each(2, lambda i: head_tile(i + 2))

    inv_row = jnp.concatenate([info1[i, 0:1] for i in range(4)], axis=1)
    for i in range(4):
        unit = jnp.transpose(xblk[i].astype(F32)) * info1[i, 0:1]
        ut[:, pl.ds(i * 128, 128)] = unit
    gain_col = jnp.transpose(jnp.broadcast_to(gains[1:2, block_cols(block)], (128, 128)))
    statc[pl.ds(0, 128), :] = gain_col

    start_b(g)
    start_b(other)
    start_c(g)
    start_c(other)
    finish(g)
    finish(other)

    mine16 = pl.ds(pl.multiple_of(lax.rem(vs, 8) * 16, 16), 16)
    gain16 = statc[mine16, 0:1]
    gain_total = jnp.zeros((16, 1), F32)
    for h in range(2):
        cols = pl.ds(h * 256, 256)
        unit = ut[mine16, cols]
        grad = fin[h]
        row_mean = rt_s[h, 2][1:2] * (SOFTEN_TEMP / 4096)
        hidden = inv_row[:, h * 256 : h * 256 + 256] * (grad * gain16 - unit * row_mean)
        hidden_out[:, cols] = hidden.astype(BF16)
        gain_total += jnp.sum(grad * unit, axis=1, keepdims=True)
    wide = jnp.concatenate([jnp.broadcast_to(gain_total, (16, 128)), jnp.zeros((112, 128), F32)], axis=0)
    gain_out[...] = jnp.transpose(wide)[0:1, 0:16]
    loss_out[...] = lossrt[lax.div(s, 2), 0:1, pl.ds(pl.multiple_of(lax.rem(s, 2) * 128, 128), 128)]

    for kind in range(3):
        each(3, lambda i, kind=kind: x_copy(kind, i + 1, True).wait_send())

    def sent_yz(i):
        info_copy(i + 1, True).wait_send()
        for k in range(2):
            y_copy(k, i + 1, True).wait_send()
            y_relay(k, i + 1, True).wait_send()
        each(7, lambda j: z_copy(j + 1, i + 1, True).wait_send())

    each(3, sent_yz)

    @pl.when(g == 1)
    def _():
        w_copy().wait_send()
        xblk_copy.wait_send()
        info_pair.wait_send()
        n1_copy.wait_send()

    for axis, count in ((0, 3), (1, 3), (2, 7)):
        each(count, lambda i, axis=axis: st_copy(axis, i + 1).wait_send())

    def sent_ab(h):
        def one(i):
            at_copy(h, i + 1).wait_send()
            b_copy(h, i + 1).wait_send()
            bt_copy(h, i + 1).wait_send()

        def two(i):
            c_copy(h, i + 1).wait_send()
            ct_copy(h, i + 1).wait_send()

        for part in range(3):
            for k in range(2):
                a_copy(h, k, part).wait_send()
        each(3, one)
        each(7, two)

    each(2, sent_ab)


def per_device(hidden_states, output_head_weights, norm_gains, label_ids):
    dma = pltpu.SemaphoreType.DMA
    vm = pltpu.VMEM
    scratch = [
        vm((4, 128, 4096), BF16),
        vm((512, 4096), BF16),
        vm((4096, 896), BF16),
        vm((2048, 896), BF16),
        vm((512, 2048), BF16),
        vm((2048, 512), BF16),
        vm((512, 896), F32),
        vm((256, 896), F32),
        vm((256, 896), F32),
        vm((256, 896), F32),
        vm((256, 896), F32),
        vm((512, 896), BF16),
        vm((4, 8, 128), F32),
        vm((4, 8, 128), F32),
        vm((4, 128, 128), F32),
        vm((512, 128), F32),
        vm((2, 4096), F32),
        vm((1, 128), jnp.int32),
        vm((4, 128, 128), BF16),
        vm((128, 512), F32),
        vm((256, 128), F32),
        vm((3, 8, 256), F32),
        vm((13, 8, 256), F32),
        vm((2, 8, 256), F32),
        vm((256, 128), F32),
        vm((2, 4, 4, 8, 16, 256), BF16),
        vm((2, 2, 2, 8, 16, 256), BF16),
        vm((2, 2, 2, 8, 16, 256), BF16),
        vm((2, 2, 4, 8, 16, 256), BF16),
        vm((2, 4, 8, 16, 256), BF16),
        vm((2, 3, 8, 16, 256), BF16),
        vm((2, 8, 16, 256), BF16),
        vm((2, 7, 16, 256), BF16),
        vm((2, 3, 8, 256), F32),
        vm((2, 3, 8, 256), F32),
        vm((2, 3, 8, 256), F32),
        vm((2, 7, 8, 256), F32),
        vm((2, 16, 256), F32),
        dma((8,)),
        dma((3, 3)), dma((3, 3)),
        dma((4, 3)), dma((4, 3)),
        dma((7, 3)), dma((7, 3)),
        dma((3,)), dma((3,)),
        dma((7,)), dma((7,)),
        dma((2, 3)), dma((2, 3)),
        dma((7,)), dma((7,)),
        dma((2, 5, 3)), dma((2, 5, 3)),
        dma((2, 2, 7)), dma((2, 2, 7)),
    ]
    whole = pl.BlockSpec(memory_space=pltpu.HBM)
    vmem = pl.BlockSpec(memory_space=pltpu.VMEM)
    loss, head_grad, hidden_grad, gain_grad = pl.pallas_call(
        kernel,
        name="distill",
        out_shape=(
            vm((1, 128), F32),
            vm((2048, 896), BF16),
            vm((16, 512), BF16),
            vm((1, 16), F32),
        ),
        in_specs=[whole] * 4,
        out_specs=(vmem,) * 4,
        scratch_shapes=scratch,
        cost_estimate=pl.CostEstimate(flops=10**10, bytes_accessed=2 * 10**7, transcendentals=10**6),
        compiler_params=pltpu.CompilerParams(
            collective_id=0, has_side_effects=True, vmem_limit_bytes=50 * 2**20
        ),
    )(hidden_states, output_head_weights, norm_gains, label_ids.reshape(1, 128))
    return loss.reshape(128), head_grad, hidden_grad, gain_grad.reshape(16)


def solution(mesh):
    placed = (P("grp", "seq", None), P("grp", None, ("vocab", "seq")), P(), P("seq"))
    return jax.shard_map(
        per_device,
        mesh=mesh,
        in_specs=placed,
        out_specs=(
            P("seq"),
            P("grp", ("vocab", "seq")),
            P(("grp", "vocab", "seq"), None),
            P(("grp", "vocab", "seq")),
        ),
        check_vma=False,
    )
```

```python
import jax
import jax.numpy as jnp
from jax import lax
from jax.experimental import pallas as pl
from jax.experimental.pallas import tpu as pltpu
from jax.sharding import PartitionSpec as P

SOFTEN_TEMP = 2.0
LABEL_WEIGHT = 0.5
EPSILON = 1e-06
MESH = pl.DeviceIdType.MESH
F32, BF16 = jnp.float32, jnp.bfloat16
NX, NY, NZ = 4, 4, 8
Y_SUB, Z_SUB = 512, 128
Z_BASE = NY * Y_SUB
X_BASE = Z_BASE + NZ * Z_SUB
ROWS = 32
PEERS = [(0, 0, d) for d in (1, 2, 3)] + [(0, d, 0) for d in (1, 2, 3)] + [(d, 0, 0) for d in range(1, 8)]


def each(count, body):
    def step(i, carry):
        body(i)
        return carry

    lax.fori_loop(0, count, step, 0)


def kernel(
    hs, w_hbm, gains_hbm, label_hbm,
    loss_out, head_out, hidden_out, gain_out,
    xg, nrm, w, w1h, n1h, n1t, z, zp, e0s, e1s, z1s, lg,
    info, info1, invb, labb, gains, label, xblk, ut,
    statc, st_send, st_recv, lossrt, colb,
    ng, q1, q2, r1, s2, r2, s3, r3, rt_s, rt_r1, rt_r2, rt_r3, fin,
    loc, xs_s, xs_r, ys_s, ys_r, zs_s, zs_r, in_s, in_r, pr_s, pr_r,
    sa_s, sa_r, sz_s, sz_r, ab_s, ab_r, cz_s, cz_r,
):
    g = lax.axis_index("grp")
    v = lax.axis_index("vocab")
    s = lax.axis_index("seq")
    zc = lax.div(v, NY)
    yc = lax.rem(v, NY)
    other = 1 - g
    is_teacher = g == 0

    def device(dz, dy, dx):
        return {
            "grp": g,
            "vocab": lax.rem(zc + dz, NZ) * NY + lax.rem(yc + dy, NY),
            "seq": lax.rem(s + dx, NX),
        }

    partner = {"grp": other, "vocab": v, "seq": s}

    def remote(src, dst, ssem, rsem, to):
        return pltpu.make_async_remote_copy(
            src_ref=src, dst_ref=dst, send_sem=ssem, recv_sem=rsem, device_id=to, device_id_type=MESH
        )

    load_x = pltpu.make_async_copy(hs.at[0], xg.at[s], loc.at[0])
    load_g = pltpu.make_async_copy(gains_hbm, gains, loc.at[1])
    load_l = pltpu.make_async_copy(label_hbm, label, loc.at[2])
    load_w = pltpu.make_async_copy(w_hbm.at[0], w, loc.at[3])
    load_x.start()
    load_g.start()
    load_l.start()

    barrier = pltpu.get_barrier_semaphore()
    for dz, dy, dx in PEERS:
        pl.semaphore_signal(barrier, inc=1, device_id=device(dz, dy, dx), device_id_type=MESH)
    pl.semaphore_signal(barrier, inc=1, device_id=partner, device_id_type=MESH)
    pl.semaphore_wait(barrier, len(PEERS) + 1)

    def y_cols(y, part):
        return pl.ds(pl.multiple_of(y * Y_SUB + part * 256, 256), 256)

    def y_half(y, part, k):
        return pl.ds(pl.multiple_of(y * Y_SUB + part * 256 + k * 128, 128), 128)

    def z_cols(at):
        return pl.ds(pl.multiple_of(Z_BASE + at * Z_SUB, 128), Z_SUB)

    def x_copy(kind, d, to):
        cols = (z_cols(zc), y_cols(yc, 0), y_cols(yc, 1), pl.ds(X_BASE, 1024))[kind]
        at = s if to else lax.rem(s + NX - d, NX)
        dst = xg.at[at, :, cols]
        return remote(
            hs.at[0, :, cols] if to else dst, dst, xs_s.at[kind, d - 1], xs_r.at[kind, d - 1], device(0, 0, d)
        )

    def x_relay(k, to):
        d = 1 + 2 * k
        ref = xg.at[lax.rem(s + (NX - d if to else 2), NX), :, pl.ds(X_BASE + 512 * k, 512)]
        return remote(ref, ref, xs_s.at[4, k], xs_r.at[4, k], device(0, 0, d))

    def info_copy(d, to):
        at = s if to else lax.rem(s + NX - d, NX)
        return remote(info.at[at], info.at[at], in_s.at[d - 1], in_r.at[d - 1], device(0, 0, d))

    for kind in range(3):
        each(3, lambda i, kind=kind: x_copy(kind, i + 1, True).start())
    load_w.start()

    half_w = pl.ds(0, 2048)

    def w_copy():
        return remote(w_hbm.at[0, half_w, :], w1h, pr_s.at[0], pr_r.at[0], partner)

    load_w1 = pltpu.make_async_copy(w_hbm.at[0, pl.ds(2048, 2048), :], w1h, loc.at[4])

    @pl.when(g == 1)
    def _():
        w_copy().start()
        load_w1.start()

    load_x.wait()
    load_g.wait()
    load_l.wait()
    total = jnp.zeros((128, 128), F32)
    for b in range(32):
        part = xg[s, :, pl.ds(b * 128, 128)].astype(F32)
        total += part * part
    mean = jnp.sum(total, axis=1, keepdims=True) * (1.0 / 4096)
    inverse = lax.rsqrt(mean + EPSILON)
    inverse_rows = jnp.transpose(jnp.broadcast_to(inverse, (128, 128)))[0:8]
    sub8 = lax.broadcasted_iota(jnp.int32, (8, 128), 0)
    label_rows = jnp.broadcast_to(label[...].astype(F32), (8, 128))
    info[s] = jnp.where(sub8 == 1, label_rows, inverse_rows)

    each(3, lambda i: info_copy(i + 1, True).start())

    def y_copy(part, k, d, to):
        shard = lax.rem(s + NX - d, NX)
        dy = 1 + 2 * k
        ref = xg.at[shard, :, y_cols(yc if to else lax.rem(yc + NY - dy, NY), part)]
        return remote(ref, ref, ys_s.at[part, k, d - 1], ys_r.at[part, k, d - 1], device(0, dy, 0))

    def y_relay(part, k, d, to):
        shard = lax.rem(s + NX - d, NX)
        dy = 1 + 2 * k
        ref = xg.at[shard, :, y_half(lax.rem(yc + (NY - dy if to else 2), NY), part, k)]
        return remote(ref, ref, ys_s.at[part, 2 + k, d - 1], ys_r.at[part, 2 + k, d - 1], device(0, dy, 0))

    def z_copy(slot, d, to):
        shard = lax.rem(s + NX - d, NX)
        k = slot % 2
        hops = (2, 1, 1, 2)[slot // 2]
        far = (2, 1, 3, 4)[slot // 2]
        step = NZ - hops if k else hops
        away = far if k else NZ - far
        at = lax.rem(zc + (away + step) % NZ, NZ) if to else lax.rem(zc + away, NZ)
        rows = pl.ds(64 * k, 64) if slot >= 6 else pl.ds(0, 128)
        ref = xg.at[shard, rows, z_cols(at)]
        return remote(ref, ref, zs_s.at[slot, d - 1], zs_r.at[slot, d - 1], device(step, 0, 0))

    def forward_z(i):
        x_copy(0, i + 1, False).wait_recv()
        for slot in range(4):
            z_copy(slot, i + 1, True).start()

    def pass_z(i):
        for k in range(2):
            z_copy(k, i + 1, False).wait_recv()
            z_copy(4 + k, i + 1, True).start()
            z_copy(6 + k, i + 1, True).start()

    def forward_y(part, i):
        x_copy(1 + part, i + 1, False).wait_recv()
        for k in range(2):
            y_copy(part, k, i + 1, True).start()

    def pass_y(part, i):
        for k in range(2):
            y_copy(part, k, i + 1, False).wait_recv()
            y_relay(part, k, i + 1, True).start()

    each(3, forward_z)
    each(3, lambda i: forward_y(0, i))
    each(3, lambda i: forward_y(1, i))
    for k in range(2):
        x_copy(3, 1 + 2 * k, True).start()
    each(3, pass_z)
    each(3, lambda i: pass_y(0, i))

    each(3, lambda i: info_copy(i + 1, False).wait_recv())
    tall = jnp.transpose(jnp.concatenate([info[i] for i in range(4)] + [jnp.zeros((96, 128), F32)], axis=0))
    for i in range(4):
        invb[i] = jnp.broadcast_to(tall[:, 8 * i : 8 * i + 1], (128, 128))
        labb[pl.ds(128 * i, 128), :] = jnp.broadcast_to(tall[:, 8 * i + 1 : 8 * i + 2], (128, 128))
    load_w.wait()

    def normalized(f0, width):
        for b in range(width // 128):
            cols = pl.ds(pl.multiple_of(f0 + b * 128, 128), 128)
            gain = jnp.where(is_teacher, gains[0:1, cols], gains[1:2, cols])
            for i in range(4):
                unit = xg[i, :, cols].astype(F32) * invb[i]
                nrm[pl.ds(i * 128, 128), cols] = (unit * gain).astype(BF16)

    def accumulate(f0, width, first=False):
        normalized(f0, width)
        cols = pl.ds(pl.multiple_of(f0, 128), width)
        product = jnp.dot(nrm[:, cols], w[cols, :], preferred_element_type=F32)
        if first:
            z[...] = product
        else:
            z[...] += product

    accumulate(yc * Y_SUB, Y_SUB, first=True)
    each(3, lambda i: pass_y(1, i))
    for k in range(2):
        x_copy(3, 1 + 2 * k, False).wait_recv()
        x_relay(k, True).start()

    def add_y(i):
        accumulate(lax.rem(yc + 1 + 2 * i, NY) * Y_SUB, Y_SUB)

    each(2, add_y)

    def take_z(i):
        for slot in range(2, 8):
            z_copy(slot, i + 1, False).wait_recv()

    each(3, take_z)
    accumulate(Z_BASE, 512)
    accumulate(Z_BASE + 512, 512)

    def take_y(i):
        for part in range(2):
            for k in range(2):
                y_relay(part, k, i + 1, False).wait_recv()

    each(3, take_y)
    accumulate(lax.rem(yc + 2, NY) * Y_SUB, Y_SUB)
    x_relay(0, False).wait_recv()
    accumulate(X_BASE, 512)
    x_relay(1, False).wait_recv()

    own = pl.ds(pl.multiple_of(g * 256, 256), 256)
    theirs = pl.ds(pl.multiple_of(other * 256, 256), 256)
    halves = ((0, 512), (512, 384))

    def z_trade(k):
        cols = pl.ds(*halves[k])
        return remote(z.at[theirs, cols], zp.at[:, cols], pr_s.at[(1, 7)[k]], pr_r.at[(1, 7)[k]], partner)

    normalized(X_BASE + 512, 512)
    for k in range(2):
        last = pl.ds(X_BASE + 512, 512)
        cols = pl.ds(*halves[k])
        z[:, cols] += jnp.dot(nrm[:, last], w[last, cols], preferred_element_type=F32)
        z_trade(k).start()

    vs = v * NX + s
    teacher_block = lax.div(vs, 8)
    block = g * 16 + teacher_block

    def block_cols(b):
        return pl.ds(pl.multiple_of(b * 128, 128), 128)

    xblk_copy = remote(xg.at[:, :, block_cols(teacher_block)], xblk, pr_s.at[2], pr_r.at[2], partner)
    info_pair = remote(info, info1, pr_s.at[3], pr_r.at[3], partner)
    n1_copy = remote(nrm.at[:, half_w], n1h, pr_s.at[4], pr_r.at[4], partner)
    own_block = pltpu.make_async_copy(xg.at[:, :, block_cols(block)], xblk, loc.at[5])
    own_info = pltpu.make_async_copy(info, info1, loc.at[6])
    own_n1 = pltpu.make_async_copy(nrm.at[:, pl.ds(2048, 2048)], n1h, loc.at[7])

    for k in range(2):
        z_trade(k).wait()

    @pl.when(g == 1)
    def _():
        xblk_copy.start()
        info_pair.start()
        n1_copy.start()
        own_block.start()
        own_info.start()
        own_n1.start()

    lane = lax.broadcasted_iota(jnp.int32, (ROWS, 128), 1)
    column = lax.broadcasted_iota(jnp.int32, (ROWS, 896), 1)

    def labels_at(r):
        rows = pl.ds(pl.multiple_of(g * 256 + r * ROWS, ROWS), ROWS)
        return labb[rows, 0:1].astype(jnp.int32) - vs * 896

    def totals(r):
        rows = pl.ds(pl.multiple_of(r * ROWS, ROWS), ROWS)
        mine = z[pl.ds(pl.multiple_of(g * 256 + r * ROWS, ROWS), ROWS), :] * (1.0 / SOFTEN_TEMP)
        given = zp[rows, :] * (1.0 / SOFTEN_TEMP)
        z0 = jnp.where(is_teacher, mine, given)
        z1 = jnp.where(is_teacher, given, mine)
        m0 = jnp.max(z0, axis=1, keepdims=True)
        m1 = jnp.max(z1, axis=1, keepdims=True)
        e0 = jnp.exp(z0 - m0)
        e1 = jnp.exp(z1 - m1)
        e0s[rows, :] = e0
        e1s[rows, :] = e1
        z1s[rows, :] = z1
        t0 = jnp.sum(e0, axis=1, keepdims=True)
        t1 = jnp.sum(e1, axis=1, keepdims=True)
        cross = jnp.sum(e0 * (z0 - z1), axis=1, keepdims=True)
        picked = jnp.sum(jnp.where(column == labels_at(r), z1, 0.0), axis=1, keepdims=True)
        stats = jnp.zeros((ROWS, 128), F32)
        for i, value in enumerate((m0, t0, cross, m1, t1, picked)):
            stats = jnp.where(lane == i, value, stats)
        statc[rows, :] = stats

    each(256 // ROWS, totals)
    local = jnp.transpose(statc[...])[0:8]
    st_send[0] = local

    def merge(parts):
        m0 = parts[0][0:1]
        m1 = parts[0][3:4]
        for p in parts[1:]:
            m0 = jnp.maximum(m0, p[0:1])
            m1 = jnp.maximum(m1, p[3:4])
        t0 = cross = t1 = picked = jnp.zeros((1, 256), F32)
        for p in parts:
            s0 = jnp.exp(p[0:1] - m0)
            s1 = jnp.exp(p[3:4] - m1)
            t0 += s0 * p[1:2]
            cross += s0 * p[2:3]
            t1 += s1 * p[4:5]
            picked += p[5:6]
        return jnp.concatenate([m0, t0, cross, m1, t1, picked, picked, picked], axis=0)

    def st_copy(axis, d):
        to = device(0, 0, d) if axis == 0 else device(0, d, 0) if axis == 1 else device(d, 0, 0)
        sems = (sz_s.at[d - 1], sz_r.at[d - 1]) if axis == 2 else (sa_s.at[axis, d - 1], sa_r.at[axis, d - 1])
        return remote(st_send.at[axis], st_recv.at[axis * 3 + d - 1], *sems, to)

    merged = local
    for axis, count in ((0, 3), (1, 3), (2, 7)):
        if axis:
            st_send[axis] = merged
        each(count, lambda i, axis=axis: st_copy(axis, i + 1).start())
        each(count, lambda i, axis=axis: st_copy(axis, i + 1).wait_recv())
        merged = merge([merged] + [st_recv[axis * 3 + i] for i in range(count)])

    lse0 = merged[0:1] + jnp.log(merged[1:2])
    lse1 = merged[3:4] + jnp.log(merged[4:5])
    loss = merged[2:3] / merged[1:2] - lse0 + lse1 + LABEL_WEIGHT * (lse1 - merged[5:6])
    scale = 128 * 896 / 16.0 / SOFTEN_TEMP
    a0 = scale * jnp.exp(local[0:1] - lse0)
    a1 = (scale * (1.0 + LABEL_WEIGHT)) * jnp.exp(local[3:4] - lse1)
    colb[...] = jnp.transpose(jnp.concatenate([a0, a1, jnp.zeros((126, 256), F32)], axis=0))

    def gradient(r):
        rows = pl.ds(pl.multiple_of(r * ROWS, ROWS), ROWS)
        cols = colb[rows, :]
        target = jnp.where(column == labels_at(r), scale * LABEL_WEIGHT, 0.0)
        grad = (cols[:, 1:2] * e1s[rows, :] - cols[:, 0:1] * e0s[rows, :] - target).astype(BF16)
        lg[pl.ds(pl.multiple_of(g * 256 + r * ROWS, ROWS), ROWS), :] = grad
        along = jnp.sum(grad.astype(F32) * z1s[rows, :], axis=1, keepdims=True)
        statc[rows, :] = jnp.broadcast_to(along, (ROWS, 128))

    each(256 // ROWS, gradient)
    lg_trade = remote(lg.at[own, :], lg.at[own, :], pr_s.at[5], pr_r.at[5], partner)
    lg_trade.start()

    @pl.when(g == 0)
    def _():
        w_copy().wait_recv()

    @pl.when(g == 1)
    def _():
        load_w1.wait()

    def states_grad(h):
        tokens = lg[pl.ds(pl.multiple_of(h * 256, 256), 256), :]

        def tile(i):
            rows = w1h[pl.ds(pl.multiple_of(i * 512, 512), 512), :]
            product = lax.dot_general(rows, tokens, (((1,), (1,)), ((), ())), preferred_element_type=F32)
            for k in range(2):
                for y in range(NY):
                    for x in range(NX):
                        at = k * 256 + (y * NX + x) * 16
                        a = x + (y - x) * h
                        b = y + (x - y) * h
                        ng[h, a, b, 2 * i + k] = product[at : at + 16].astype(BF16)

        each(4, tile)

    def first(h):
        return s + (yc - s) * h

    def second(h):
        return yc + (s - yc) * h

    def a_copy(h, k, part):
        d = 1 + 2 * k
        to = device(0, d * h, d * (1 - h))
        blocks = pl.ds(2 * ((k + part) % 2), 2)
        sems = (ab_s.at[h, k, part], ab_r.at[h, k, part])
        if part == 0:
            return remote(ng.at[h, lax.rem(first(h) + 2, 4), blocks], q1.at[h, k], *sems, to)
        src = ng.at[h, lax.rem(first(h) + d, 4), blocks] if part == 1 else q2.at[h, k]
        return remote(src, r1.at[h, k, blocks], *sems, to)

    def at_copy(h, d):
        to = device(0, d * h, d * (1 - h))
        return remote(lossrt.at[h], rt_r1.at[h, d - 1], ab_s.at[h, 2, d - 1], ab_r.at[h, 2, d - 1], to)

    def b_copy(h, d):
        to = device(0, d * (1 - h), d * h)
        return remote(s2.at[h, lax.rem(second(h) + d, 4)], r2.at[h, d - 1], ab_s.at[h, 3, d - 1], ab_r.at[h, 3, d - 1], to)

    def bt_copy(h, d):
        to = device(0, d * (1 - h), d * h)
        return remote(rt_s.at[h, 0], rt_r2.at[h, d - 1], ab_s.at[h, 4, d - 1], ab_r.at[h, 4, d - 1], to)

    def c_copy(h, d):
        return remote(s3.at[h, lax.rem(zc + d, NZ)], r3.at[h, d - 1], cz_s.at[h, 0, d - 1], cz_r.at[h, 0, d - 1], device(d, 0, 0))

    def ct_copy(h, d):
        return remote(rt_s.at[h, 1], rt_r3.at[h, d - 1], cz_s.at[h, 1, d - 1], cz_r.at[h, 1, d - 1], device(d, 0, 0))

    def start_a(h):
        for part in range(2):
            for k in range(2):
                a_copy(h, k, part).start()

    def start_at(h):
        each(3, lambda i: at_copy(h, i + 1).start())

    def pass_a(h):
        for k in range(2):
            a_copy(h, k, 0).wait_recv()
            at = lax.rem(first(h) + 1 + 2 * k, 4)

            def add(i, k=k, at=at):
                for b in range(2):
                    q2[h, k, b, i] = (ng[h, at, 2 * k + b, i].astype(F32) + q1[h, k, b, i].astype(F32)).astype(BF16)

            each(NZ, add)
            a_copy(h, k, 2).start()

    def start_b(h):
        each(3, lambda i: at_copy(h, i + 1).wait_recv())
        for k in range(2):
            a_copy(h, k, 1).wait_recv()
            a_copy(h, k, 2).wait_recv()
        mine = first(h)

        def add(b):
            for k in range(NZ):
                total = ng[h, mine, b, k].astype(F32)
                for i in range(2):
                    total += r1[h, i, b, k].astype(F32)
                s2[h, b, k] = total.astype(BF16)

        each(4, add)
        rt_s[h, 0] = lossrt[h] + rt_r1[h, 0] + rt_r1[h, 1] + rt_r1[h, 2]

        def go(i):
            b_copy(h, i + 1).start()
            bt_copy(h, i + 1).start()

        each(3, go)

    def start_c(h):
        def got(i):
            b_copy(h, i + 1).wait_recv()
            bt_copy(h, i + 1).wait_recv()

        each(3, got)
        mine = second(h)
        for k in range(NZ):
            total = s2[h, mine, k].astype(F32)
            for i in range(3):
                total += r2[h, i, k].astype(F32)
            s3[h, k] = total.astype(BF16)
        rt_s[h, 1] = rt_s[h, 0] + rt_r2[h, 0] + rt_r2[h, 1] + rt_r2[h, 2]

        def go(i):
            c_copy(h, i + 1).start()
            ct_copy(h, i + 1).start()

        each(7, go)

    def finish(h):
        def got(i):
            c_copy(h, i + 1).wait_recv()
            ct_copy(h, i + 1).wait_recv()

        each(7, got)
        total = s3[h, zc].astype(F32)
        along = rt_s[h, 1]
        for i in range(7):
            total += r3[h, i].astype(F32)
            along += rt_r3[h, i]
        fin[h] = total
        rt_s[h, 2] = along

    states_grad(g)
    start_a(g)
    lg_trade.wait_recv()
    states_grad(other)
    start_a(other)

    along_row = jnp.transpose(statc[...])[0:8]
    sub8w = lax.broadcasted_iota(jnp.int32, (8, 256), 0)
    lossrt[g] = jnp.where(sub8w == 0, jnp.broadcast_to(loss, (8, 256)), along_row)
    rt_trade = remote(lossrt.at[g], lossrt.at[g], pr_s.at[6], pr_r.at[6], partner)
    rt_trade.start()

    start_at(g)
    rt_trade.wait()
    lg_trade.wait_send()
    start_at(other)

    @pl.when(g == 0)
    def _():
        n1_copy.wait_recv()
        xblk_copy.wait_recv()
        info_pair.wait_recv()

    @pl.when(g == 1)
    def _():
        own_n1.wait()
        own_block.wait()
        own_info.wait()

    def flip(i):
        cols = pl.ds(pl.multiple_of(i * 128, 128), 128)
        n1t[cols, :] = jnp.transpose(n1h[:, cols])

    each(16, flip)

    pass_a(g)

    def head_tile(i):
        rows = pl.ds(pl.multiple_of(i * 512, 512), 512)
        head_out[rows, :] = jnp.dot(n1t[rows, :], lg[...], preferred_element_type=F32).astype(BF16)

    each(2, head_tile)
    pass_a(other)
    each(2, lambda i: head_tile(i + 2))

    inv_row = jnp.concatenate([info1[i, 0:1] for i in range(4)], axis=1)
    for i in range(4):
        unit = jnp.transpose(xblk[i].astype(F32)) * info1[i, 0:1]
        ut[:, pl.ds(i * 128, 128)] = unit
    gain_col = jnp.transpose(jnp.broadcast_to(gains[1:2, block_cols(block)], (128, 128)))
    statc[pl.ds(0, 128), :] = gain_col

    start_b(g)
    start_b(other)
    start_c(g)
    start_c(other)
    finish(g)
    finish(other)

    mine16 = pl.ds(pl.multiple_of(lax.rem(vs, 8) * 16, 16), 16)
    gain16 = statc[mine16, 0:1]
    gain_total = jnp.zeros((16, 1), F32)
    for h in range(2):
        cols = pl.ds(h * 256, 256)
        unit = ut[mine16, cols]
        grad = fin[h]
        row_mean = rt_s[h, 2][1:2] * (SOFTEN_TEMP / 4096)
        hidden = inv_row[:, h * 256 : h * 256 + 256] * (grad * gain16 - unit * row_mean)
        hidden_out[:, cols] = hidden.astype(BF16)
        gain_total += jnp.sum(grad * unit, axis=1, keepdims=True)
    wide = jnp.concatenate([jnp.broadcast_to(gain_total, (16, 128)), jnp.zeros((112, 128), F32)], axis=0)
    gain_out[...] = jnp.transpose(wide)[0:1, 0:16]
    loss_out[...] = lossrt[lax.div(s, 2), 0:1, pl.ds(pl.multiple_of(lax.rem(s, 2) * 128, 128), 128)]

    for kind in range(3):
        each(3, lambda i, kind=kind: x_copy(kind, i + 1, True).wait_send())
    for k in range(2):
        x_copy(3, 1 + 2 * k, True).wait_send()
        x_relay(k, True).wait_send()

    def sent_yz(i):
        info_copy(i + 1, True).wait_send()
        for part in range(2):
            for k in range(2):
                y_copy(part, k, i + 1, True).wait_send()
                y_relay(part, k, i + 1, True).wait_send()
        for slot in range(8):
            z_copy(slot, i + 1, True).wait_send()

    each(3, sent_yz)

    @pl.when(g == 1)
    def _():
        w_copy().wait_send()
        xblk_copy.wait_send()
        info_pair.wait_send()
        n1_copy.wait_send()

    for axis, count in ((0, 3), (1, 3), (2, 7)):
        each(count, lambda i, axis=axis: st_copy(axis, i + 1).wait_send())

    def sent_ab(h):
        def one(i):
            at_copy(h, i + 1).wait_send()
            b_copy(h, i + 1).wait_send()
            bt_copy(h, i + 1).wait_send()

        def two(i):
            c_copy(h, i + 1).wait_send()
            ct_copy(h, i + 1).wait_send()

        for part in range(3):
            for k in range(2):
                a_copy(h, k, part).wait_send()
        each(3, one)
        each(7, two)

    each(2, sent_ab)


def store(loss, head, hidden, gain, loss_out, head_out, hidden_out, gain_out, sems):
    pairs = ((head, head_out), (hidden, hidden_out), (loss, loss_out), (gain, gain_out))
    copies = [pltpu.make_async_copy(a, b, sems.at[i]) for i, (a, b) in enumerate(pairs)]
    for copy in copies:
        copy.start()
    for copy in copies:
        copy.wait()


def per_device(hidden_states, output_head_weights, norm_gains, label_ids):
    dma = pltpu.SemaphoreType.DMA
    vm = pltpu.VMEM
    scratch = [
        vm((4, 128, 4096), BF16),
        vm((512, 4096), BF16),
        vm((4096, 896), BF16),
        vm((2048, 896), BF16),
        vm((512, 2048), BF16),
        vm((2048, 512), BF16),
        vm((512, 896), F32),
        vm((256, 896), F32),
        vm((256, 896), F32),
        vm((256, 896), F32),
        vm((256, 896), F32),
        vm((512, 896), BF16),
        vm((4, 8, 128), F32),
        vm((4, 8, 128), F32),
        vm((4, 128, 128), F32),
        vm((512, 128), F32),
        vm((2, 4096), F32),
        vm((1, 128), jnp.int32),
        vm((4, 128, 128), BF16),
        vm((128, 512), F32),
        vm((256, 128), F32),
        vm((3, 8, 256), F32),
        vm((13, 8, 256), F32),
        vm((2, 8, 256), F32),
        vm((256, 128), F32),
        vm((2, 4, 4, 8, 16, 256), BF16),
        vm((2, 2, 2, 8, 16, 256), BF16),
        vm((2, 2, 2, 8, 16, 256), BF16),
        vm((2, 2, 4, 8, 16, 256), BF16),
        vm((2, 4, 8, 16, 256), BF16),
        vm((2, 3, 8, 16, 256), BF16),
        vm((2, 8, 16, 256), BF16),
        vm((2, 7, 16, 256), BF16),
        vm((2, 3, 8, 256), F32),
        vm((2, 3, 8, 256), F32),
        vm((2, 3, 8, 256), F32),
        vm((2, 7, 8, 256), F32),
        vm((2, 16, 256), F32),
        dma((8,)),
        dma((5, 3)), dma((5, 3)),
        dma((2, 4, 3)), dma((2, 4, 3)),
        dma((8, 3)), dma((8, 3)),
        dma((3,)), dma((3,)),
        dma((8,)), dma((8,)),
        dma((2, 3)), dma((2, 3)),
        dma((7,)), dma((7,)),
        dma((2, 5, 3)), dma((2, 5, 3)),
        dma((2, 2, 7)), dma((2, 2, 7)),
    ]
    whole = pl.BlockSpec(memory_space=pltpu.HBM)
    vmem = pl.BlockSpec(memory_space=pltpu.VMEM)
    loss, head_grad, hidden_grad, gain_grad = pl.pallas_call(
        kernel,
        name="distill",
        out_shape=(
            vm((1, 128), F32),
            vm((2048, 896), BF16),
            vm((16, 512), BF16),
            vm((1, 16), F32),
        ),
        in_specs=[whole] * 4,
        out_specs=(vmem,) * 4,
        scratch_shapes=scratch,
        cost_estimate=pl.CostEstimate(flops=10**10, bytes_accessed=2 * 10**7, transcendentals=10**6),
        compiler_params=pltpu.CompilerParams(
            collective_id=0, has_side_effects=True, vmem_limit_bytes=59 * 2**20
        ),
    )(hidden_states, output_head_weights, norm_gains, label_ids.reshape(1, 128))
    loss, head_grad, hidden_grad, gain_grad = pl.pallas_call(
        store,
        name="store",
        out_shape=[jax.ShapeDtypeStruct(a.shape, a.dtype) for a in (loss, head_grad, hidden_grad, gain_grad)],
        in_specs=[vmem] * 4,
        out_specs=[pl.BlockSpec(memory_space=pltpu.HBM)] * 4,
        scratch_shapes=[dma((4,))],
    )(loss, head_grad, hidden_grad, gain_grad)
    return loss.reshape(128), head_grad, hidden_grad, gain_grad.reshape(16)


def solution(mesh):
    placed = (P("grp", "seq", None), P("grp", None, ("vocab", "seq")), P(), P("seq"))
    return jax.shard_map(
        per_device,
        mesh=mesh,
        in_specs=placed,
        out_specs=(
            P("seq"),
            P("grp", ("vocab", "seq")),
            P(("grp", "vocab", "seq"), None),
            P(("grp", "vocab", "seq")),
        ),
        check_vma=False,
    )
```

```python
import jax
import jax.numpy as jnp
from jax import lax
from jax.experimental import pallas as pl
from jax.experimental.pallas import tpu as pltpu
from jax.sharding import PartitionSpec as P

SOFTEN_TEMP = 2.0
LABEL_WEIGHT = 0.5
EPSILON = 1e-06
MESH = pl.DeviceIdType.MESH
F32, BF16 = jnp.float32, jnp.bfloat16
NX, NY, NZ = 4, 4, 8
Y_SUB, Z_SUB = 512, 128
Z_BASE = NY * Y_SUB
X_BASE = Z_BASE + NZ * Z_SUB
ROWS = 32
PEERS = [(0, 0, d) for d in (1, 2, 3)] + [(0, d, 0) for d in (1, 2, 3)] + [(d, 0, 0) for d in range(1, 8)]


def each(count, body):
    def step(i, carry):
        body(i)
        return carry

    lax.fori_loop(0, count, step, 0)


def kernel(
    hs, w_hbm, gains_hbm, label_hbm,
    loss_out, head_out, hidden_out, gain_out,
    xg, nrm, w, w1h, n1h, n1t, z, zp, e_own, e_given, lg,
    info, info1, invb, labb, gains, label, xblk, ut,
    statc, st_send, st_recv, losses, colb, gainb,
    ng, q1, q2, r1, s2, r2, s3, r3, rt_s, rt_r1, rt_r2, rt_r3, fin,
    loc, xs_s, xs_r, ys_s, ys_r, zs_s, zs_r, in_s, in_r, pr_s, pr_r,
    sa_s, sa_r, sz_s, sz_r, ab_s, ab_r, cz_s, cz_r,
):
    g = lax.axis_index("grp")
    v = lax.axis_index("vocab")
    s = lax.axis_index("seq")
    zc = lax.div(v, NY)
    yc = lax.rem(v, NY)
    other = 1 - g
    is_teacher = g == 0

    def device(dz, dy, dx):
        return {
            "grp": g,
            "vocab": lax.rem(zc + dz, NZ) * NY + lax.rem(yc + dy, NY),
            "seq": lax.rem(s + dx, NX),
        }

    partner = {"grp": other, "vocab": v, "seq": s}

    def remote(src, dst, ssem, rsem, to):
        return pltpu.make_async_remote_copy(
            src_ref=src, dst_ref=dst, send_sem=ssem, recv_sem=rsem, device_id=to, device_id_type=MESH
        )

    load_x = pltpu.make_async_copy(hs.at[0], xg.at[s], loc.at[0])
    load_g = pltpu.make_async_copy(gains_hbm, gains, loc.at[1])
    load_l = pltpu.make_async_copy(label_hbm, label, loc.at[2])
    load_w = pltpu.make_async_copy(w_hbm.at[0], w, loc.at[3])
    load_x.start()
    load_g.start()
    load_l.start()

    barrier = pltpu.get_barrier_semaphore()
    for dz, dy, dx in PEERS:
        pl.semaphore_signal(barrier, inc=1, device_id=device(dz, dy, dx), device_id_type=MESH)
    pl.semaphore_signal(barrier, inc=1, device_id=partner, device_id_type=MESH)
    pl.semaphore_wait(barrier, len(PEERS) + 1)

    def y_cols(y, part):
        return pl.ds(pl.multiple_of(y * Y_SUB + part * 256, 256), 256)

    def y_half(y, part, k):
        return pl.ds(pl.multiple_of(y * Y_SUB + part * 256 + k * 128, 128), 128)

    def z_cols(at):
        return pl.ds(pl.multiple_of(Z_BASE + at * Z_SUB, 128), Z_SUB)

    def x_copy(kind, d, to):
        cols = (z_cols(zc), y_cols(yc, 0), y_cols(yc, 1), pl.ds(X_BASE, 1024))[kind]
        at = s if to else lax.rem(s + NX - d, NX)
        dst = xg.at[at, :, cols]
        return remote(
            hs.at[0, :, cols] if to else dst, dst, xs_s.at[kind, d - 1], xs_r.at[kind, d - 1], device(0, 0, d)
        )

    def x_relay(k, to):
        d = 1 + 2 * k
        ref = xg.at[lax.rem(s + (NX - d if to else 2), NX), :, pl.ds(X_BASE + 512 * k, 512)]
        return remote(ref, ref, xs_s.at[4, k], xs_r.at[4, k], device(0, 0, d))

    def info_copy(d, to):
        at = s if to else lax.rem(s + NX - d, NX)
        return remote(info.at[at], info.at[at], in_s.at[d - 1], in_r.at[d - 1], device(0, 0, d))

    def x_start(kind):
        each(3, lambda i: x_copy(kind, i + 1, True).start())

    x_start(0)
    x_start(1)
    load_w.start()

    half_w = pl.ds(0, 2048)

    def w_copy():
        return remote(w_hbm.at[0, half_w, :], w1h, pr_s.at[0], pr_r.at[0], partner)

    load_w1 = pltpu.make_async_copy(w_hbm.at[0, pl.ds(2048, 2048), :], w1h, loc.at[4])

    @pl.when(g == 1)
    def _():
        w_copy().start()
        load_w1.start()

    load_x.wait()
    load_g.wait()
    load_l.wait()
    total = jnp.zeros((128, 128), F32)
    for b in range(32):
        part = xg[s, :, pl.ds(b * 128, 128)].astype(F32)
        total += part * part
    mean = jnp.sum(total, axis=1, keepdims=True) * (1.0 / 4096)
    inverse = lax.rsqrt(mean + EPSILON)
    inverse_rows = jnp.transpose(jnp.broadcast_to(inverse, (128, 128)))[0:8]
    sub8 = lax.broadcasted_iota(jnp.int32, (8, 128), 0)
    label_rows = jnp.broadcast_to(label[...].astype(F32), (8, 128))
    info[s] = jnp.where(sub8 == 1, label_rows, inverse_rows)

    each(3, lambda i: info_copy(i + 1, True).start())

    def y_copy(part, k, d, to):
        shard = lax.rem(s + NX - d, NX)
        dy = 1 + 2 * k
        ref = xg.at[shard, :, y_cols(yc if to else lax.rem(yc + NY - dy, NY), part)]
        return remote(ref, ref, ys_s.at[part, k, d - 1], ys_r.at[part, k, d - 1], device(0, dy, 0))

    def y_relay(part, k, d, to):
        shard = lax.rem(s + NX - d, NX)
        dy = 1 + 2 * k
        ref = xg.at[shard, :, y_half(lax.rem(yc + (NY - dy if to else 2), NY), part, k)]
        return remote(ref, ref, ys_s.at[part, 2 + k, d - 1], ys_r.at[part, 2 + k, d - 1], device(0, dy, 0))

    def z_copy(slot, d, to):
        shard = lax.rem(s + NX - d, NX)
        k = slot % 2
        hops = (2, 1, 1, 2)[slot // 2]
        far = (2, 1, 3, 4)[slot // 2]
        step = NZ - hops if k else hops
        away = far if k else NZ - far
        at = lax.rem(zc + (away + step) % NZ, NZ) if to else lax.rem(zc + away, NZ)
        rows = pl.ds(64 * k, 64) if slot >= 6 else pl.ds(0, 128)
        ref = xg.at[shard, rows, z_cols(at)]
        return remote(ref, ref, zs_s.at[slot, d - 1], zs_r.at[slot, d - 1], device(step, 0, 0))

    def forward_z(i):
        x_copy(0, i + 1, False).wait_recv()
        for slot in range(4):
            z_copy(slot, i + 1, True).start()

    def pass_z(i):
        for k in range(2):
            z_copy(k, i + 1, False).wait_recv()
            z_copy(4 + k, i + 1, True).start()
            z_copy(6 + k, i + 1, True).start()

    def forward_y(part, i):
        x_copy(1 + part, i + 1, False).wait_recv()
        for k in range(2):
            y_copy(part, k, i + 1, True).start()

    def pass_y(part, i):
        for k in range(2):
            y_copy(part, k, i + 1, False).wait_recv()
            y_relay(part, k, i + 1, True).start()

    each(3, forward_z)
    x_start(2)
    each(3, lambda i: forward_y(0, i))
    for k in range(2):
        x_copy(3, 1 + 2 * k, True).start()
    each(3, lambda i: forward_y(1, i))
    each(3, pass_z)
    each(3, lambda i: pass_y(0, i))

    each(3, lambda i: info_copy(i + 1, False).wait_recv())
    tall = jnp.transpose(jnp.concatenate([info[i] for i in range(4)] + [jnp.zeros((96, 128), F32)], axis=0))
    for i in range(4):
        invb[i] = jnp.broadcast_to(tall[:, 8 * i : 8 * i + 1], (128, 128))
        labb[pl.ds(128 * i, 128), :] = jnp.broadcast_to(tall[:, 8 * i + 1 : 8 * i + 2], (128, 128))
    load_w.wait()

    def normalized(f0, width):
        for b in range(width // 128):
            cols = pl.ds(pl.multiple_of(f0 + b * 128, 128), 128)
            gain = jnp.where(is_teacher, gains[0:1, cols], gains[1:2, cols])
            for i in range(4):
                unit = xg[i, :, cols].astype(F32) * invb[i]
                nrm[pl.ds(i * 128, 128), cols] = (unit * gain).astype(BF16)

    def accumulate(f0, width, first=False):
        normalized(f0, width)
        cols = pl.ds(pl.multiple_of(f0, 128), width)
        product = jnp.dot(nrm[:, cols], w[cols, :], preferred_element_type=F32)
        if first:
            z[...] = product
        else:
            z[...] += product

    accumulate(yc * Y_SUB, Y_SUB, first=True)
    each(3, lambda i: pass_y(1, i))
    for k in range(2):
        x_copy(3, 1 + 2 * k, False).wait_recv()
        x_relay(k, True).start()

    def add_y(i):
        accumulate(lax.rem(yc + 1 + 2 * i, NY) * Y_SUB, Y_SUB)

    each(2, add_y)

    def take_z(i):
        for slot in range(2, 8):
            z_copy(slot, i + 1, False).wait_recv()

    each(3, take_z)
    accumulate(Z_BASE, 512)
    accumulate(Z_BASE + 512, 512)

    def take_y(i):
        for part in range(2):
            for k in range(2):
                y_relay(part, k, i + 1, False).wait_recv()

    each(3, take_y)
    accumulate(lax.rem(yc + 2, NY) * Y_SUB, Y_SUB)
    x_relay(0, False).wait_recv()
    accumulate(X_BASE, 512)
    x_relay(1, False).wait_recv()

    own = pl.ds(pl.multiple_of(g * 256, 256), 256)
    theirs = pl.ds(pl.multiple_of(other * 256, 256), 256)
    halves = ((0, 512), (512, 384))

    def z_trade(k):
        cols = pl.ds(*halves[k])
        return remote(z.at[theirs, cols], zp.at[:, cols], pr_s.at[(1, 7)[k]], pr_r.at[(1, 7)[k]], partner)

    normalized(X_BASE + 512, 512)
    for k in range(2):
        last = pl.ds(X_BASE + 512, 512)
        cols = pl.ds(*halves[k])
        z[:, cols] += jnp.dot(nrm[:, last], w[last, cols], preferred_element_type=F32)
        z_trade(k).start()

    lane = lax.broadcasted_iota(jnp.int32, (ROWS, 128), 1)
    column = lax.broadcasted_iota(jnp.int32, (ROWS, 896), 1)
    vs = v * NX + s

    def half_rows(r):
        return pl.ds(pl.multiple_of(r * ROWS, ROWS), ROWS)

    def own_rows(r):
        return pl.ds(pl.multiple_of(g * 256 + r * ROWS, ROWS), ROWS)

    def labels_at(r):
        return labb[own_rows(r), 0:1].astype(jnp.int32) - vs * 896

    def own_totals(r):
        rows = half_rows(r)
        mine = z[own_rows(r), :] * (1.0 / SOFTEN_TEMP)
        top = jnp.max(mine, axis=1, keepdims=True)
        e = jnp.exp(mine - top)
        e_own[rows, :] = e
        total = jnp.sum(e, axis=1, keepdims=True)
        statc[rows, :] = jnp.where(lane == 0, top, jnp.broadcast_to(total, (ROWS, 128)))

    each(256 // ROWS, own_totals)
    teacher_block = lax.div(vs, 8)
    block = g * 16 + teacher_block

    def block_cols(b):
        return pl.ds(pl.multiple_of(b * 128, 128), 128)

    xblk_copy = remote(xg.at[:, :, block_cols(teacher_block)], xblk, pr_s.at[2], pr_r.at[2], partner)
    info_pair = remote(info, info1, pr_s.at[3], pr_r.at[3], partner)
    n1_copy = remote(nrm.at[:, half_w], n1h, pr_s.at[4], pr_r.at[4], partner)
    own_block = pltpu.make_async_copy(xg.at[:, :, block_cols(block)], xblk, loc.at[5])
    own_info = pltpu.make_async_copy(info, info1, loc.at[6])
    own_n1 = pltpu.make_async_copy(nrm.at[:, pl.ds(2048, 2048)], n1h, loc.at[7])

    for k in range(2):
        z_trade(k).wait()


    @pl.when(g == 1)
    def _():
        xblk_copy.start()
        info_pair.start()
        n1_copy.start()
        own_block.start()
        own_info.start()
        own_n1.start()

    def totals(r):
        rows = half_rows(r)
        mine = z[own_rows(r), :] * (1.0 / SOFTEN_TEMP)
        given = zp[rows, :] * (1.0 / SOFTEN_TEMP)
        top = jnp.max(given, axis=1, keepdims=True)
        e = jnp.exp(given - top)
        e_given[rows, :] = e
        total = jnp.sum(e, axis=1, keepdims=True)
        e0 = jnp.where(is_teacher, e_own[rows, :], e)
        gap = jnp.where(is_teacher, mine - given, given - mine)
        cross = jnp.sum(e0 * gap, axis=1, keepdims=True)
        z1 = jnp.where(is_teacher, given, mine)
        picked = jnp.sum(jnp.where(column == labels_at(r), z1, 0.0), axis=1, keepdims=True)
        stats = statc[rows, :]
        own_at = jnp.where(is_teacher, 0, 3)
        own_top, own_total = stats[:, 0:1], stats[:, 1:2]
        for i, value in enumerate((own_top, own_total)):
            stats = jnp.where(lane == own_at + i, value, stats)
        for i, value in enumerate((top, total)):
            stats = jnp.where(lane == 3 - own_at + i, value, stats)
        stats = jnp.where(lane == 2, cross, stats)
        statc[rows, :] = jnp.where(lane == 5, picked, stats)

    each(256 // ROWS, totals)
    local = jnp.transpose(statc[...])[0:8]
    st_send[0] = local

    def merge(parts):
        m0 = parts[0][0:1]
        m1 = parts[0][3:4]
        for p in parts[1:]:
            m0 = jnp.maximum(m0, p[0:1])
            m1 = jnp.maximum(m1, p[3:4])
        t0 = cross = t1 = picked = jnp.zeros((1, 256), F32)
        for p in parts:
            s0 = jnp.exp(p[0:1] - m0)
            s1 = jnp.exp(p[3:4] - m1)
            t0 += s0 * p[1:2]
            cross += s0 * p[2:3]
            t1 += s1 * p[4:5]
            picked += p[5:6]
        return jnp.concatenate([m0, t0, cross, m1, t1, picked, picked, picked], axis=0)

    def st_copy(axis, d):
        to = device(0, 0, d) if axis == 0 else device(0, d, 0) if axis == 1 else device(d, 0, 0)
        sems = (sz_s.at[d - 1], sz_r.at[d - 1]) if axis == 2 else (sa_s.at[axis, d - 1], sa_r.at[axis, d - 1])
        return remote(st_send.at[axis], st_recv.at[axis * 3 + d - 1], *sems, to)

    def prepare():
        @pl.when(g == 0)
        def _():
            n1_copy.wait_recv()
            xblk_copy.wait_recv()
            info_pair.wait_recv()

        @pl.when(g == 1)
        def _():
            own_n1.wait()
            own_block.wait()
            own_info.wait()

        def flip(i):
            cols = pl.ds(pl.multiple_of(i * 128, 128), 128)
            n1t[cols, :] = jnp.transpose(n1h[:, cols])

        each(16, flip)

        for i in range(4):
            unit = jnp.transpose(xblk[i].astype(F32)) * info1[i, 0:1]
            ut[:, pl.ds(i * 128, 128)] = unit
        gain_col = jnp.transpose(jnp.broadcast_to(gains[1:2, block_cols(block)], (128, 128)))
        gainb[...] = gain_col

        @pl.when(g == 0)
        def _():
            w_copy().wait_recv()

        @pl.when(g == 1)
        def _():
            load_w1.wait()

    merged = local
    for axis, count in ((0, 3), (1, 3), (2, 7)):
        if axis:
            st_send[axis] = merged
        each(count, lambda i, axis=axis: st_copy(axis, i + 1).start())
        if axis == 2:
            prepare()
        each(count, lambda i, axis=axis: st_copy(axis, i + 1).wait_recv())
        merged = merge([merged] + [st_recv[axis * 3 + i] for i in range(count)])

    lse0 = merged[0:1] + jnp.log(merged[1:2])
    lse1 = merged[3:4] + jnp.log(merged[4:5])
    loss = merged[2:3] / merged[1:2] - lse0 + lse1 + LABEL_WEIGHT * (lse1 - merged[5:6])
    losses[g] = loss
    loss_trade = remote(losses.at[g], losses.at[g], pr_s.at[8], pr_r.at[8], partner)
    scale = 128 * 896 / 16.0 / SOFTEN_TEMP
    a0 = -scale * jnp.exp(local[0:1] - lse0)
    a1 = (scale * (1.0 + LABEL_WEIGHT)) * jnp.exp(local[3:4] - lse1)
    pair = [jnp.where(is_teacher, a0, a1), jnp.where(is_teacher, a1, a0)]
    colb[...] = jnp.transpose(jnp.concatenate(pair + [jnp.zeros((126, 256), F32)], axis=0))

    def gradient(r):
        rows = half_rows(r)
        cols = colb[rows, :]
        target = jnp.where(column == labels_at(r), scale * LABEL_WEIGHT, 0.0)
        lg[own_rows(r), :] = (cols[:, 0:1] * e_own[rows, :] + cols[:, 1:2] * e_given[rows, :] - target).astype(BF16)

    each(256 // ROWS, gradient)
    lg_trade = remote(lg.at[own, :], lg.at[own, :], pr_s.at[5], pr_r.at[5], partner)
    lg_trade.start()
    loss_trade.start()

    def states_grad(h):
        tokens = lg[pl.ds(pl.multiple_of(h * 256, 256), 256), :]

        def tile(i):
            rows = w1h[pl.ds(pl.multiple_of(i * 512, 512), 512), :]
            product = lax.dot_general(rows, tokens, (((1,), (1,)), ((), ())), preferred_element_type=F32)
            for k in range(2):
                for y in range(NY):
                    for x in range(NX):
                        at = k * 256 + (y * NX + x) * 16
                        a = x + (y - x) * h
                        b = y + (x - y) * h
                        ng[h, a, b, 2 * i + k] = product[at : at + 16].astype(BF16)

        each(4, tile)

    def first(h):
        return s + (yc - s) * h

    def second(h):
        return yc + (s - yc) * h

    def a_copy(h, k, part):
        d = 1 + 2 * k
        to = device(0, d * h, d * (1 - h))
        blocks = pl.ds(2 * ((k + part) % 2), 2)
        sems = (ab_s.at[h, k, part], ab_r.at[h, k, part])
        if part == 0:
            return remote(ng.at[h, lax.rem(first(h) + 2, 4), blocks], q1.at[h, k], *sems, to)
        src = ng.at[h, lax.rem(first(h) + d, 4), blocks] if part == 1 else q2.at[h, k]
        return remote(src, r1.at[h, k, blocks], *sems, to)

    def at_copy(h, d):
        to = device(0, d * h, d * (1 - h))
        return remote(rt_s.at[h, 3], rt_r1.at[h, d - 1], ab_s.at[h, 2, d - 1], ab_r.at[h, 2, d - 1], to)

    def b_copy(h, d):
        to = device(0, d * (1 - h), d * h)
        return remote(s2.at[h, lax.rem(second(h) + d, 4)], r2.at[h, d - 1], ab_s.at[h, 3, d - 1], ab_r.at[h, 3, d - 1], to)

    def bt_copy(h, d):
        to = device(0, d * (1 - h), d * h)
        return remote(rt_s.at[h, 0], rt_r2.at[h, d - 1], ab_s.at[h, 4, d - 1], ab_r.at[h, 4, d - 1], to)

    def c_copy(h, d):
        return remote(s3.at[h, lax.rem(zc + d, NZ)], r3.at[h, d - 1], cz_s.at[h, 0, d - 1], cz_r.at[h, 0, d - 1], device(d, 0, 0))

    def ct_copy(h, d):
        return remote(rt_s.at[h, 1], rt_r3.at[h, d - 1], cz_s.at[h, 1, d - 1], cz_r.at[h, 1, d - 1], device(d, 0, 0))

    def start_a(h):
        for part in range(2):
            for k in range(2):
                a_copy(h, k, part).start()

    def start_at(h):
        each(3, lambda i: at_copy(h, i + 1).start())

    def pass_a(h):
        for k in range(2):
            a_copy(h, k, 0).wait_recv()
            at = lax.rem(first(h) + 1 + 2 * k, 4)

            def add(i, k=k, at=at):
                for b in range(2):
                    q2[h, k, b, i] = (ng[h, at, 2 * k + b, i].astype(F32) + q1[h, k, b, i].astype(F32)).astype(BF16)

            each(NZ, add)
            a_copy(h, k, 2).start()

    def start_b(h):
        each(3, lambda i: at_copy(h, i + 1).wait_recv())
        for k in range(2):
            a_copy(h, k, 1).wait_recv()
            a_copy(h, k, 2).wait_recv()
        mine = first(h)

        def add(b):
            for k in range(NZ):
                total = ng[h, mine, b, k].astype(F32)
                for i in range(2):
                    total += r1[h, i, b, k].astype(F32)
                s2[h, b, k] = total.astype(BF16)

        each(4, add)
        rt_s[h, 0] = rt_s[h, 3] + rt_r1[h, 0] + rt_r1[h, 1] + rt_r1[h, 2]

        def go(i):
            b_copy(h, i + 1).start()
            bt_copy(h, i + 1).start()

        each(3, go)

    def start_c(h):
        def got(i):
            b_copy(h, i + 1).wait_recv()
            bt_copy(h, i + 1).wait_recv()

        each(3, got)
        mine = second(h)
        for k in range(NZ):
            total = s2[h, mine, k].astype(F32)
            for i in range(3):
                total += r2[h, i, k].astype(F32)
            s3[h, k] = total.astype(BF16)
        rt_s[h, 1] = rt_s[h, 0] + rt_r2[h, 0] + rt_r2[h, 1] + rt_r2[h, 2]

        def go(i):
            c_copy(h, i + 1).start()
            ct_copy(h, i + 1).start()

        each(7, go)

    def finish(h):
        def got(i):
            c_copy(h, i + 1).wait_recv()
            ct_copy(h, i + 1).wait_recv()

        each(7, got)
        total = s3[h, zc].astype(F32)
        along = rt_s[h, 1]
        for i in range(7):
            total += r3[h, i].astype(F32)
            along += rt_r3[h, i]
        fin[h] = total
        rt_s[h, 2] = along

    states_grad(g)
    start_a(g)
    lg_trade.wait_recv()
    states_grad(other)
    start_a(other)

    def along(r):
        rows = pl.ds(pl.multiple_of(r * ROWS, ROWS), ROWS)
        grad = lg[pl.ds(pl.multiple_of(g * 256 + r * ROWS, ROWS), ROWS), :].astype(F32)
        z1 = jnp.where(is_teacher, zp[rows, :], z[pl.ds(pl.multiple_of(g * 256 + r * ROWS, ROWS), ROWS), :])
        total = jnp.sum(grad * z1, axis=1, keepdims=True) * (1.0 / SOFTEN_TEMP)
        statc[rows, :] = jnp.broadcast_to(total, (ROWS, 128))

    each(256 // ROWS, along)
    rt_s[g, 3] = jnp.transpose(statc[...])[0:1]
    rt_trade = remote(rt_s.at[g, 3], rt_s.at[g, 3], pr_s.at[6], pr_r.at[6], partner)
    rt_trade.start()
    start_at(g)
    rt_trade.wait()
    lg_trade.wait_send()
    loss_trade.wait()
    start_at(other)

    def head_tile(i):
        rows = pl.ds(pl.multiple_of(i * 512, 512), 512)
        head_out[rows, :] = jnp.dot(n1t[rows, :], lg[...], preferred_element_type=F32).astype(BF16)

    each(2, head_tile)
    pass_a(g)
    head_tile(2)
    pass_a(other)
    head_tile(3)

    start_b(g)
    start_b(other)
    start_c(g)
    start_c(other)
    finish(g)
    finish(other)

    inv_row = jnp.concatenate([info1[i, 0:1] for i in range(4)], axis=1)
    mine16 = pl.ds(pl.multiple_of(lax.rem(vs, 8) * 16, 16), 16)
    gain16 = gainb[mine16, 0:1]
    gain_total = jnp.zeros((16, 1), F32)
    for h in range(2):
        cols = pl.ds(h * 256, 256)
        unit = ut[mine16, cols]
        grad = fin[h]
        row_mean = rt_s[h, 2] * (SOFTEN_TEMP / 4096)
        hidden = inv_row[:, h * 256 : h * 256 + 256] * (grad * gain16 - unit * row_mean)
        hidden_out[:, cols] = hidden.astype(BF16)
        gain_total += jnp.sum(grad * unit, axis=1, keepdims=True)
    wide = jnp.concatenate([jnp.broadcast_to(gain_total, (16, 128)), jnp.zeros((112, 128), F32)], axis=0)
    gain_out[...] = jnp.transpose(wide)[0:1, 0:16]
    loss_out[...] = losses[lax.div(s, 2), :, pl.ds(pl.multiple_of(lax.rem(s, 2) * 128, 128), 128)]

    for kind in range(3):
        each(3, lambda i, kind=kind: x_copy(kind, i + 1, True).wait_send())
    for k in range(2):
        x_copy(3, 1 + 2 * k, True).wait_send()
        x_relay(k, True).wait_send()

    def sent_yz(i):
        info_copy(i + 1, True).wait_send()
        for part in range(2):
            for k in range(2):
                y_copy(part, k, i + 1, True).wait_send()
                y_relay(part, k, i + 1, True).wait_send()
        for slot in range(8):
            z_copy(slot, i + 1, True).wait_send()

    each(3, sent_yz)

    @pl.when(g == 1)
    def _():
        w_copy().wait_send()
        xblk_copy.wait_send()
        info_pair.wait_send()
        n1_copy.wait_send()

    for axis, count in ((0, 3), (1, 3), (2, 7)):
        each(count, lambda i, axis=axis: st_copy(axis, i + 1).wait_send())

    def sent_ab(h):
        def one(i):
            at_copy(h, i + 1).wait_send()
            b_copy(h, i + 1).wait_send()
            bt_copy(h, i + 1).wait_send()

        def two(i):
            c_copy(h, i + 1).wait_send()
            ct_copy(h, i + 1).wait_send()

        for part in range(3):
            for k in range(2):
                a_copy(h, k, part).wait_send()
        each(3, one)
        each(7, two)

    each(2, sent_ab)


def store(loss, head, hidden, gain, loss_out, head_out, hidden_out, gain_out, sems):
    pairs = ((head, head_out), (hidden, hidden_out), (loss, loss_out), (gain, gain_out))
    copies = [pltpu.make_async_copy(a, b, sems.at[i]) for i, (a, b) in enumerate(pairs)]
    for copy in copies:
        copy.start()
    for copy in copies:
        copy.wait()


def per_device(hidden_states, output_head_weights, norm_gains, label_ids):
    dma = pltpu.SemaphoreType.DMA
    vm = pltpu.VMEM
    scratch = [
        vm((4, 128, 4096), BF16),
        vm((512, 4096), BF16),
        vm((4096, 896), BF16),
        vm((2048, 896), BF16),
        vm((512, 2048), BF16),
        vm((2048, 512), BF16),
        vm((512, 896), F32),
        vm((256, 896), F32),
        vm((256, 896), F32),
        vm((256, 896), F32),
        vm((512, 896), BF16),
        vm((4, 8, 128), F32),
        vm((4, 8, 128), F32),
        vm((4, 128, 128), F32),
        vm((512, 128), F32),
        vm((2, 4096), F32),
        vm((1, 128), jnp.int32),
        vm((4, 128, 128), BF16),
        vm((128, 512), F32),
        vm((256, 128), F32),
        vm((3, 8, 256), F32),
        vm((13, 8, 256), F32),
        vm((2, 1, 256), F32),
        vm((256, 128), F32),
        vm((128, 128), F32),
        vm((2, 4, 4, 8, 16, 256), BF16),
        vm((2, 2, 2, 8, 16, 256), BF16),
        vm((2, 2, 2, 8, 16, 256), BF16),
        vm((2, 2, 4, 8, 16, 256), BF16),
        vm((2, 4, 8, 16, 256), BF16),
        vm((2, 3, 8, 16, 256), BF16),
        vm((2, 8, 16, 256), BF16),
        vm((2, 7, 16, 256), BF16),
        vm((2, 4, 1, 256), F32),
        vm((2, 3, 1, 256), F32),
        vm((2, 3, 1, 256), F32),
        vm((2, 7, 1, 256), F32),
        vm((2, 16, 256), F32),
        dma((8,)),
        dma((5, 3)), dma((5, 3)),
        dma((2, 4, 3)), dma((2, 4, 3)),
        dma((8, 3)), dma((8, 3)),
        dma((3,)), dma((3,)),
        dma((9,)), dma((9,)),
        dma((2, 3)), dma((2, 3)),
        dma((7,)), dma((7,)),
        dma((2, 5, 3)), dma((2, 5, 3)),
        dma((2, 2, 7)), dma((2, 2, 7)),
    ]
    whole = pl.BlockSpec(memory_space=pltpu.HBM)
    vmem = pl.BlockSpec(memory_space=pltpu.VMEM)
    loss, head_grad, hidden_grad, gain_grad = pl.pallas_call(
        kernel,
        name="distill",
        out_shape=(
            vm((1, 128), F32),
            vm((2048, 896), BF16),
            vm((16, 512), BF16),
            vm((1, 16), F32),
        ),
        in_specs=[whole] * 4,
        out_specs=(vmem,) * 4,
        scratch_shapes=scratch,
        cost_estimate=pl.CostEstimate(flops=10**10, bytes_accessed=2 * 10**7, transcendentals=10**6),
        compiler_params=pltpu.CompilerParams(
            collective_id=0, has_side_effects=True, vmem_limit_bytes=59 * 2**20
        ),
    )(hidden_states, output_head_weights, norm_gains, label_ids.reshape(1, 128))
    loss, head_grad, hidden_grad, gain_grad = pl.pallas_call(
        store,
        name="store",
        out_shape=[jax.ShapeDtypeStruct(a.shape, a.dtype) for a in (loss, head_grad, hidden_grad, gain_grad)],
        in_specs=[vmem] * 4,
        out_specs=[pl.BlockSpec(memory_space=pltpu.HBM)] * 4,
        scratch_shapes=[dma((4,))],
        compiler_params=pltpu.CompilerParams(vmem_limit_bytes=4 * 2**20),
    )(loss, head_grad, hidden_grad, gain_grad)
    return loss.reshape(128), head_grad, hidden_grad, gain_grad.reshape(16)


def solution(mesh):
    placed = (P("grp", "seq", None), P("grp", None, ("vocab", "seq")), P(), P("seq"))
    return jax.shard_map(
        per_device,
        mesh=mesh,
        in_specs=placed,
        out_specs=(
            P("seq"),
            P("grp", ("vocab", "seq")),
            P(("grp", "vocab", "seq"), None),
            P(("grp", "vocab", "seq")),
        ),
        check_vma=False,
    )
```

```python
import jax
import jax.numpy as jnp
from jax import lax
from jax.experimental import pallas as pl
from jax.experimental.pallas import tpu as pltpu
from jax.sharding import PartitionSpec as P

SOFTEN_TEMP = 2.0
LABEL_WEIGHT = 0.5
EPSILON = 1e-06
MESH = pl.DeviceIdType.MESH
F32, BF16 = jnp.float32, jnp.bfloat16
NX, NY, NZ = 4, 4, 8
Y_SUB, Z_SUB = 512, 128
Z_BASE = NY * Y_SUB
X_BASE = Z_BASE + NZ * Z_SUB
ROWS = 128
PEERS = [(0, 0, d) for d in (1, 2, 3)] + [(0, d, 0) for d in (1, 2, 3)] + [(d, 0, 0) for d in range(1, 8)]


def each(count, body):
    def step(i, carry):
        body(i)
        return carry

    lax.fori_loop(0, count, step, 0)


def kernel(
    hs, w_hbm, gains_hbm, label_hbm,
    loss_out, head_out, hidden_out, gain_out,
    xg, nrm, w, w1h, n1h, n1t, z, zp, e_own, e_given, lg,
    info, info1, invb, labb, gains, label, xblk, ut,
    statc, st_send, st_recv, losses, colb, gainb,
    ng, q1, q2, r1, s2, r2, s3, r3, rt_s, rt_r, rt_other, fin,
    loc, xs_s, xs_r, ys_s, ys_r, zs_s, zs_r, in_s, in_r, pr_s, pr_r,
    sa_s, sa_r, sz_s, sz_r, ab_s, ab_r, cz_s, cz_r, rt_sem,
):
    g = lax.axis_index("grp")
    v = lax.axis_index("vocab")
    s = lax.axis_index("seq")
    zc = lax.div(v, NY)
    yc = lax.rem(v, NY)
    other = 1 - g
    is_teacher = g == 0

    def device(dz, dy, dx):
        return {
            "grp": g,
            "vocab": lax.rem(zc + dz, NZ) * NY + lax.rem(yc + dy, NY),
            "seq": lax.rem(s + dx, NX),
        }

    partner = {"grp": other, "vocab": v, "seq": s}

    def remote(src, dst, ssem, rsem, to):
        return pltpu.make_async_remote_copy(
            src_ref=src, dst_ref=dst, send_sem=ssem, recv_sem=rsem, device_id=to, device_id_type=MESH
        )

    load_x = pltpu.make_async_copy(hs.at[0], xg.at[s], loc.at[0])
    load_g = pltpu.make_async_copy(gains_hbm, gains, loc.at[1])
    load_l = pltpu.make_async_copy(label_hbm, label, loc.at[2])
    load_w = pltpu.make_async_copy(w_hbm.at[0], w, loc.at[3])
    load_x.start()
    load_g.start()
    load_l.start()

    barrier = pltpu.get_barrier_semaphore()
    for dz, dy, dx in PEERS:
        pl.semaphore_signal(barrier, inc=1, device_id=device(dz, dy, dx), device_id_type=MESH)
    pl.semaphore_signal(barrier, inc=1, device_id=partner, device_id_type=MESH)
    pl.semaphore_wait(barrier, len(PEERS) + 1)

    def y_cols(y, part):
        return pl.ds(pl.multiple_of(y * Y_SUB + part * 256, 256), 256)

    def y_half(y, part, k):
        return pl.ds(pl.multiple_of(y * Y_SUB + part * 256 + k * 128, 128), 128)

    def z_cols(at):
        return pl.ds(pl.multiple_of(Z_BASE + at * Z_SUB, 128), Z_SUB)

    def x_copy(kind, d, to):
        cols = (z_cols(zc), y_cols(yc, 0), y_cols(yc, 1))[kind]
        at = s if to else lax.rem(s + NX - d, NX)
        dst = xg.at[at, :, cols]
        return remote(
            dst, dst, xs_s.at[kind, d - 1], xs_r.at[kind, d - 1], device(0, 0, d)
        )

    def x_near(part, k, to):
        d = 1 + 2 * k
        cols = pl.ds(X_BASE + 512 * (k if part == 0 else 1 - k), 512)
        at = s if to else lax.rem(s + NX - d, NX)
        dst = xg.at[at, :, cols]
        return remote(dst, dst, xs_s.at[3 + part, k], xs_r.at[3 + part, k], device(0, 0, d))

    def x_relay(k, to):
        d = 1 + 2 * k
        ref = xg.at[lax.rem(s + (NX - d if to else 2), NX), :, pl.ds(X_BASE + 512 * k, 512)]
        return remote(ref, ref, xs_s.at[5, k], xs_r.at[5, k], device(0, 0, d))

    def info_copy(d, to):
        at = s if to else lax.rem(s + NX - d, NX)
        return remote(info.at[at], info.at[at], in_s.at[d - 1], in_r.at[d - 1], device(0, 0, d))

    def x_start(kind):
        each(3, lambda i: x_copy(kind, i + 1, True).start())

    load_x.wait()
    x_start(0)
    x_start(1)
    x_start(2)
    load_w.start()

    half_w = pl.ds(0, 2048)

    def w_copy():
        return remote(w_hbm.at[0, half_w, :], w1h, pr_s.at[0], pr_r.at[0], partner)

    load_w1 = pltpu.make_async_copy(w_hbm.at[0, pl.ds(2048, 2048), :], w1h, loc.at[4])

    @pl.when(g == 1)
    def _():
        w_copy().start()
        load_w1.start()

    load_g.wait()
    load_l.wait()
    total = jnp.zeros((128, 128), F32)
    for b in range(32):
        part = xg[s, :, pl.ds(b * 128, 128)].astype(F32)
        total += part * part
    mean = jnp.sum(total, axis=1, keepdims=True) * (1.0 / 4096)
    inverse = lax.rsqrt(mean + EPSILON)
    inverse_rows = jnp.transpose(jnp.broadcast_to(inverse, (128, 128)))[0:8]
    sub8 = lax.broadcasted_iota(jnp.int32, (8, 128), 0)
    label_rows = jnp.broadcast_to(label[...].astype(F32), (8, 128))
    info[s] = jnp.where(sub8 == 1, label_rows, inverse_rows)

    each(3, lambda i: info_copy(i + 1, True).start())

    def y_copy(part, k, d, to):
        shard = lax.rem(s + NX - d, NX)
        dy = 1 + 2 * k
        ref = xg.at[shard, :, y_cols(yc if to else lax.rem(yc + NY - dy, NY), part)]
        return remote(ref, ref, ys_s.at[part, k, d - 1], ys_r.at[part, k, d - 1], device(0, dy, 0))

    def y_relay(part, k, d, to):
        shard = lax.rem(s + NX - d, NX)
        dy = 1 + 2 * k
        ref = xg.at[shard, :, y_half(lax.rem(yc + (NY - dy if to else 2), NY), part, k)]
        return remote(ref, ref, ys_s.at[part, 2 + k, d - 1], ys_r.at[part, 2 + k, d - 1], device(0, dy, 0))

    def z_copy(slot, d, to):
        shard = lax.rem(s + NX - d, NX)
        k = slot % 2
        hops = (2, 1, 1, 2)[slot // 2]
        far = (2, 1, 3, 4)[slot // 2]
        step = NZ - hops if k else hops
        away = far if k else NZ - far
        at = lax.rem(zc + (away + step) % NZ, NZ) if to else lax.rem(zc + away, NZ)
        rows = pl.ds(64 * k, 64) if slot >= 6 else pl.ds(0, 128)
        ref = xg.at[shard, rows, z_cols(at)]
        return remote(ref, ref, zs_s.at[slot, d - 1], zs_r.at[slot, d - 1], device(step, 0, 0))

    def forward_z(i):
        x_copy(0, i + 1, False).wait_recv()
        for slot in range(4):
            z_copy(slot, i + 1, True).start()

    def pass_z(i):
        for k in range(2):
            z_copy(k, i + 1, False).wait_recv()
            z_copy(4 + k, i + 1, True).start()
            z_copy(6 + k, i + 1, True).start()

    def forward_y(part, i):
        x_copy(1 + part, i + 1, False).wait_recv()
        for k in range(2):
            y_copy(part, k, i + 1, True).start()

    def pass_y(part, i):
        for k in range(2):
            y_copy(part, k, i + 1, False).wait_recv()
            y_relay(part, k, i + 1, True).start()

    each(3, forward_z)
    each(3, lambda i: forward_y(0, i))
    for part in range(2):
        for k in range(2):
            x_near(part, k, True).start()
    each(3, lambda i: forward_y(1, i))
    each(3, pass_z)
    for k in range(2):
        x_near(0, k, False).wait_recv()
        x_relay(k, True).start()
    each(3, lambda i: pass_y(0, i))

    each(3, lambda i: info_copy(i + 1, False).wait_recv())
    tall = jnp.transpose(jnp.concatenate([info[i] for i in range(4)] + [jnp.zeros((96, 128), F32)], axis=0))
    for i in range(4):
        invb[i] = jnp.broadcast_to(tall[:, 8 * i : 8 * i + 1], (128, 128))
        labb[pl.ds(128 * i, 128), :] = jnp.broadcast_to(tall[:, 8 * i + 1 : 8 * i + 2], (128, 128))
    load_w.wait()

    def normalized(f0, width):
        for b in range(width // 128):
            cols = pl.ds(pl.multiple_of(f0 + b * 128, 128), 128)
            gain = jnp.where(is_teacher, gains[0:1, cols], gains[1:2, cols])
            for i in range(4):
                unit = xg[i, :, cols].astype(F32) * invb[i]
                nrm[pl.ds(i * 128, 128), cols] = (unit * gain).astype(BF16)

    def accumulate(f0, width, first=False):
        normalized(f0, width)
        cols = pl.ds(pl.multiple_of(f0, 128), width)
        product = jnp.dot(nrm[:, cols], w[cols, :], preferred_element_type=F32)
        if first:
            z[...] = product
        else:
            z[...] += product

    accumulate(yc * Y_SUB, Y_SUB, first=True)
    each(3, lambda i: pass_y(1, i))

    def add_y(i):
        accumulate(lax.rem(yc + 1 + 2 * i, NY) * Y_SUB, Y_SUB)

    each(2, add_y)

    def take_z(i):
        for slot in range(2, 8):
            z_copy(slot, i + 1, False).wait_recv()

    each(3, take_z)
    accumulate(Z_BASE, 512)
    accumulate(Z_BASE + 512, 512)

    def take_y(i):
        for part in range(2):
            for k in range(2):
                y_relay(part, k, i + 1, False).wait_recv()

    each(3, take_y)
    accumulate(lax.rem(yc + 2, NY) * Y_SUB, Y_SUB)
    for k in range(2):
        x_near(1, k, False).wait_recv()
    x_relay(0, False).wait_recv()
    accumulate(X_BASE, 512)
    x_relay(1, False).wait_recv()

    own = pl.ds(pl.multiple_of(g * 256, 256), 256)
    theirs = pl.ds(pl.multiple_of(other * 256, 256), 256)
    halves = ((0, 512), (512, 384))

    def z_trade(k):
        cols = pl.ds(*halves[k])
        return remote(z.at[theirs, cols], zp.at[:, cols], pr_s.at[(1, 7)[k]], pr_r.at[(1, 7)[k]], partner)

    normalized(X_BASE + 512, 512)
    for k in range(2):
        last = pl.ds(X_BASE + 512, 512)
        cols = pl.ds(*halves[k])
        z[:, cols] += jnp.dot(nrm[:, last], w[last, cols], preferred_element_type=F32)
        z_trade(k).start()

    lane = lax.broadcasted_iota(jnp.int32, (ROWS, 128), 1)
    column = lax.broadcasted_iota(jnp.int32, (ROWS, 896), 1)
    vs = v * NX + s

    def half_rows(r):
        return pl.ds(pl.multiple_of(r * ROWS, ROWS), ROWS)

    def own_rows(r):
        return pl.ds(pl.multiple_of(g * 256 + r * ROWS, ROWS), ROWS)

    def labels_at(r):
        return labb[own_rows(r), 0:1].astype(jnp.int32) - vs * 896

    def own_totals(r):
        rows = half_rows(r)
        mine = z[own_rows(r), :] * (1.0 / SOFTEN_TEMP)
        top = jnp.max(mine, axis=1, keepdims=True)
        e = jnp.exp(mine - top)
        e_own[rows, :] = e
        total = jnp.sum(e, axis=1, keepdims=True)
        statc[rows, :] = jnp.where(lane == 0, top, jnp.broadcast_to(total, (ROWS, 128)))

    each(256 // ROWS, own_totals)
    teacher_block = lax.div(vs, 8)
    block = g * 16 + teacher_block

    def block_cols(b):
        return pl.ds(pl.multiple_of(b * 128, 128), 128)

    xblk_copy = remote(xg.at[:, :, block_cols(teacher_block)], xblk, pr_s.at[2], pr_r.at[2], partner)
    info_pair = remote(info, info1, pr_s.at[3], pr_r.at[3], partner)
    n1_copy = remote(nrm.at[:, half_w], n1h, pr_s.at[4], pr_r.at[4], partner)
    own_block = pltpu.make_async_copy(xg.at[:, :, block_cols(block)], xblk, loc.at[5])
    own_info = pltpu.make_async_copy(info, info1, loc.at[6])
    own_n1 = pltpu.make_async_copy(nrm.at[:, pl.ds(2048, 2048)], n1h, loc.at[7])

    for k in range(2):
        z_trade(k).wait()


    @pl.when(g == 1)
    def _():
        xblk_copy.start()
        info_pair.start()
        n1_copy.start()
        own_block.start()
        own_info.start()
        own_n1.start()

    def totals(r):
        rows = half_rows(r)
        mine = z[own_rows(r), :] * (1.0 / SOFTEN_TEMP)
        given = zp[rows, :] * (1.0 / SOFTEN_TEMP)
        top = jnp.max(given, axis=1, keepdims=True)
        e = jnp.exp(given - top)
        e_given[rows, :] = e
        total = jnp.sum(e, axis=1, keepdims=True)
        e0 = jnp.where(is_teacher, e_own[rows, :], e)
        gap = jnp.where(is_teacher, mine - given, given - mine)
        cross = jnp.sum(e0 * gap, axis=1, keepdims=True)
        z1 = jnp.where(is_teacher, given, mine)
        picked = jnp.sum(jnp.where(column == labels_at(r), z1, 0.0), axis=1, keepdims=True)
        stats = statc[rows, :]
        own_at = jnp.where(is_teacher, 0, 3)
        own_top, own_total = stats[:, 0:1], stats[:, 1:2]
        for i, value in enumerate((own_top, own_total)):
            stats = jnp.where(lane == own_at + i, value, stats)
        for i, value in enumerate((top, total)):
            stats = jnp.where(lane == 3 - own_at + i, value, stats)
        stats = jnp.where(lane == 2, cross, stats)
        statc[rows, :] = jnp.where(lane == 5, picked, stats)

    each(256 // ROWS, totals)
    local = jnp.transpose(statc[...])[0:8]
    st_send[0] = local

    def merge(parts):
        m0 = parts[0][0:1]
        m1 = parts[0][3:4]
        for p in parts[1:]:
            m0 = jnp.maximum(m0, p[0:1])
            m1 = jnp.maximum(m1, p[3:4])
        t0 = cross = t1 = picked = jnp.zeros((1, 256), F32)
        for p in parts:
            s0 = jnp.exp(p[0:1] - m0)
            s1 = jnp.exp(p[3:4] - m1)
            t0 += s0 * p[1:2]
            cross += s0 * p[2:3]
            t1 += s1 * p[4:5]
            picked += p[5:6]
        return jnp.concatenate([m0, t0, cross, m1, t1, picked, picked, picked], axis=0)

    def st_copy(axis, d):
        to = device(0, 0, d) if axis == 0 else device(0, d, 0) if axis == 1 else device(d, 0, 0)
        sems = (sz_s.at[d - 1], sz_r.at[d - 1]) if axis == 2 else (sa_s.at[axis, d - 1], sa_r.at[axis, d - 1])
        return remote(st_send.at[axis], st_recv.at[axis * 3 + d - 1], *sems, to)

    def prepare():
        @pl.when(g == 0)
        def _():
            n1_copy.wait_recv()
            xblk_copy.wait_recv()
            info_pair.wait_recv()

        @pl.when(g == 1)
        def _():
            own_n1.wait()
            own_block.wait()
            own_info.wait()

        def flip(i):
            cols = pl.ds(pl.multiple_of(i * 128, 128), 128)
            n1t[cols, :] = jnp.transpose(n1h[:, cols])

        each(16, flip)

        for i in range(4):
            unit = jnp.transpose(xblk[i].astype(F32)) * info1[i, 0:1]
            ut[:, pl.ds(i * 128, 128)] = unit
        gain_col = jnp.transpose(jnp.broadcast_to(gains[1:2, block_cols(block)], (128, 128)))
        gainb[...] = gain_col

        @pl.when(g == 0)
        def _():
            w_copy().wait_recv()

        @pl.when(g == 1)
        def _():
            load_w1.wait()

    merged = local
    for axis, count in ((0, 3), (1, 3), (2, 7)):
        if axis:
            st_send[axis] = merged
        each(count, lambda i, axis=axis: st_copy(axis, i + 1).start())
        if axis == 2:
            prepare()
        each(count, lambda i, axis=axis: st_copy(axis, i + 1).wait_recv())
        merged = merge([merged] + [st_recv[axis * 3 + i] for i in range(count)])

    lse0 = merged[0:1] + jnp.log(merged[1:2])
    lse1 = merged[3:4] + jnp.log(merged[4:5])
    loss = merged[2:3] / merged[1:2] - lse0 + lse1 + LABEL_WEIGHT * (lse1 - merged[5:6])
    losses[g] = loss
    loss_trade = remote(losses.at[g], losses.at[g], pr_s.at[8], pr_r.at[8], partner)
    scale = 128 * 896 / 16.0 / SOFTEN_TEMP
    a0 = -scale * jnp.exp(local[0:1] - lse0)
    a1 = (scale * (1.0 + LABEL_WEIGHT)) * jnp.exp(local[3:4] - lse1)
    pair = [jnp.where(is_teacher, a0, a1), jnp.where(is_teacher, a1, a0)]
    colb[...] = jnp.transpose(jnp.concatenate(pair + [jnp.zeros((126, 256), F32)], axis=0))

    def gradient(r):
        rows = half_rows(r)
        cols = colb[rows, :]
        target = jnp.where(column == labels_at(r), scale * LABEL_WEIGHT, 0.0)
        lg[own_rows(r), :] = (cols[:, 0:1] * e_own[rows, :] + cols[:, 1:2] * e_given[rows, :] - target).astype(BF16)

    each(256 // ROWS, gradient)
    lg_trade = remote(lg.at[own, :], lg.at[own, :], pr_s.at[5], pr_r.at[5], partner)
    lg_trade.start()
    loss_trade.start()

    def first(h):
        return s + (yc - s) * h

    def second(h):
        return yc + (s - yc) * h

    def a_copy(h, k, part):
        d = 1 + 2 * k
        to = device(0, d * h, d * (1 - h))
        blocks = pl.ds(2 * ((k + part) % 2), 2)
        sems = (ab_s.at[h, k, part], ab_r.at[h, k, part])
        if part == 0:
            return remote(ng.at[h, lax.rem(first(h) + 2, 4), blocks], q1.at[h, k], *sems, to)
        src = ng.at[h, lax.rem(first(h) + d, 4), blocks] if part == 1 else q2.at[h, k]
        return remote(src, r1.at[h, k, blocks], *sems, to)

    def rt_copy(step, d):
        to = (device(d, 0, 0), device(0, 0, d), device(0, d, 0))[step]
        slot = (0, 7, 10)[step] + d - 1
        return remote(rt_s.at[step], rt_r.at[slot], rt_sem.at[0, slot], rt_sem.at[1, slot], to)

    def start_rt(step):
        each((7, 3, 3)[step], lambda i: rt_copy(step, i + 1).start())

    def take_rt(step):
        count, slot = ((7, 0), (3, 7), (3, 10))[step]
        each(count, lambda i: rt_copy(step, i + 1).wait_recv())
        total = rt_s[step]
        for i in range(count):
            total += rt_r[slot + i]
        rt_s[step + 1] = total

    rt_trade = remote(rt_s.at[3], rt_other, pr_s.at[6], pr_r.at[6], partner)

    def b_copy(h, d):
        to = device(0, d * (1 - h), d * h)
        return remote(s2.at[h, lax.rem(second(h) + d, 4)], r2.at[h, d - 1], ab_s.at[h, 3, d - 1], ab_r.at[h, 3, d - 1], to)

    def c_copy(h, d):
        return remote(s3.at[h, lax.rem(zc + d, NZ)], r3.at[h, d - 1], cz_s.at[h, 0, d - 1], cz_r.at[h, 0, d - 1], device(d, 0, 0))

    def states_grad(h):
        tokens = lg[pl.ds(pl.multiple_of(h * 256, 256), 256), :]

        def shard(a):
            rows = []
            for k in range(NZ):
                for b in range(4):
                    at = k * 256 + b * (64 - 48 * h) + a * (16 + 48 * h)
                    rows.append(w1h[pl.ds(pl.multiple_of(at, 16), 16), :])
            rows = jnp.concatenate(rows, axis=0)
            product = lax.dot_general(rows, tokens, (((1,), (1,)), ((), ())), preferred_element_type=F32)
            for k in range(NZ):
                for b in range(4):
                    ng[h, a, b, k] = product[(4 * k + b) * 16 : (4 * k + b) * 16 + 16].astype(BF16)

        shard(lax.rem(first(h) + 2, 4))
        for k in range(2):
            a_copy(h, k, 0).start()
        for k in range(2):
            shard(lax.rem(first(h) + 1 + 2 * k, 4))
            a_copy(h, k, 1).start()
        shard(first(h))

    def pass_a(h):
        for k in range(2):
            a_copy(h, k, 0).wait_recv()
            at = lax.rem(first(h) + 1 + 2 * k, 4)

            def add(i, k=k, at=at):
                for b in range(2):
                    q2[h, k, b, i] = (ng[h, at, 2 * k + b, i].astype(F32) + q1[h, k, b, i].astype(F32)).astype(BF16)

            each(NZ, add)
            a_copy(h, k, 2).start()

    def start_b(h):
        for k in range(2):
            a_copy(h, k, 1).wait_recv()
            a_copy(h, k, 2).wait_recv()
        mine = first(h)

        def add(b):
            for k in range(NZ):
                total = ng[h, mine, b, k].astype(F32)
                for i in range(2):
                    total += r1[h, i, b, k].astype(F32)
                s2[h, b, k] = total.astype(BF16)

        each(4, add)

        def go(i):
            b_copy(h, i + 1).start()

        each(3, go)

    def start_c(h):
        def got(i):
            b_copy(h, i + 1).wait_recv()

        each(3, got)
        mine = second(h)
        for k in range(NZ):
            total = s2[h, mine, k].astype(F32)
            for i in range(3):
                total += r2[h, i, k].astype(F32)
            s3[h, k] = total.astype(BF16)

        def go(i):
            c_copy(h, i + 1).start()

        each(7, go)

    def finish(h):
        def got(i):
            c_copy(h, i + 1).wait_recv()

        each(7, got)
        total = s3[h, zc].astype(F32)
        for i in range(7):
            total += r3[h, i].astype(F32)
        fin[h] = total

    states_grad(g)
    lg_trade.wait_recv()
    states_grad(other)

    def along(r):
        rows = pl.ds(pl.multiple_of(r * ROWS, ROWS), ROWS)
        grad = lg[pl.ds(pl.multiple_of(g * 256 + r * ROWS, ROWS), ROWS), :].astype(F32)
        z1 = jnp.where(is_teacher, zp[rows, :], z[pl.ds(pl.multiple_of(g * 256 + r * ROWS, ROWS), ROWS), :])
        total = jnp.sum(grad * z1, axis=1, keepdims=True) * (1.0 / SOFTEN_TEMP)
        statc[rows, :] = jnp.broadcast_to(total, (ROWS, 128))

    each(256 // ROWS, along)
    rt_s[0] = jnp.transpose(statc[...])[0:1]
    start_rt(0)
    lg_trade.wait_send()
    loss_trade.wait()

    def head_tile(i):
        rows = pl.ds(pl.multiple_of(i * 512, 512), 512)
        head_out[rows, :] = jnp.dot(n1t[rows, :], lg[...], preferred_element_type=F32).astype(BF16)

    each(2, head_tile)
    pass_a(g)
    head_tile(2)
    pass_a(other)
    head_tile(3)

    start_b(g)
    start_b(other)
    take_rt(0)
    start_rt(1)
    start_c(g)
    start_c(other)
    take_rt(1)
    start_rt(2)
    take_rt(2)
    rt_trade.start()
    finish(g)
    finish(other)
    rt_trade.wait_recv()

    inv_row = jnp.concatenate([info1[i, 0:1] for i in range(4)], axis=1)
    mine16 = pl.ds(pl.multiple_of(lax.rem(vs, 8) * 16, 16), 16)
    gain16 = gainb[mine16, 0:1]
    gain_total = jnp.zeros((16, 1), F32)
    for h in range(2):
        cols = pl.ds(h * 256, 256)
        unit = ut[mine16, cols]
        grad = fin[h]
        row_mean = jnp.where(g == h, rt_s[3], rt_other[...]) * (SOFTEN_TEMP / 4096)
        hidden = inv_row[:, h * 256 : h * 256 + 256] * (grad * gain16 - unit * row_mean)
        hidden_out[:, cols] = hidden.astype(BF16)
        gain_total += jnp.sum(grad * unit, axis=1, keepdims=True)
    wide = jnp.concatenate([jnp.broadcast_to(gain_total, (16, 128)), jnp.zeros((112, 128), F32)], axis=0)
    gain_out[...] = jnp.transpose(wide)[0:1, 0:16]
    loss_out[...] = losses[lax.div(s, 2), :, pl.ds(pl.multiple_of(lax.rem(s, 2) * 128, 128), 128)]

    for kind in range(3):
        each(3, lambda i, kind=kind: x_copy(kind, i + 1, True).wait_send())
    for k in range(2):
        for part in range(2):
            x_near(part, k, True).wait_send()
        x_relay(k, True).wait_send()

    def sent_yz(i):
        info_copy(i + 1, True).wait_send()
        for part in range(2):
            for k in range(2):
                y_copy(part, k, i + 1, True).wait_send()
                y_relay(part, k, i + 1, True).wait_send()
        for slot in range(8):
            z_copy(slot, i + 1, True).wait_send()

    each(3, sent_yz)

    @pl.when(g == 1)
    def _():
        w_copy().wait_send()
        xblk_copy.wait_send()
        info_pair.wait_send()
        n1_copy.wait_send()

    for axis, count in ((0, 3), (1, 3), (2, 7)):
        each(count, lambda i, axis=axis: st_copy(axis, i + 1).wait_send())

    def sent_ab(h):
        def one(i):
            b_copy(h, i + 1).wait_send()

        def two(i):
            c_copy(h, i + 1).wait_send()

        for part in range(3):
            for k in range(2):
                a_copy(h, k, part).wait_send()
        each(3, one)
        each(7, two)

    each(2, sent_ab)
    for step, count in enumerate((7, 3, 3)):
        each(count, lambda i, step=step: rt_copy(step, i + 1).wait_send())
    rt_trade.wait_send()


def store(loss, head, hidden, gain, loss_out, head_out, hidden_out, gain_out, sems):
    pairs = ((head, head_out), (hidden, hidden_out), (loss, loss_out), (gain, gain_out))
    copies = [pltpu.make_async_copy(a, b, sems.at[i]) for i, (a, b) in enumerate(pairs)]
    for copy in copies:
        copy.start()
    for copy in copies:
        copy.wait()


def per_device(hidden_states, output_head_weights, norm_gains, label_ids):
    dma = pltpu.SemaphoreType.DMA
    vm = pltpu.VMEM
    scratch = [
        vm((4, 128, 4096), BF16),
        vm((512, 4096), BF16),
        vm((4096, 896), BF16),
        vm((2048, 896), BF16),
        vm((512, 2048), BF16),
        vm((2048, 512), BF16),
        vm((512, 896), F32),
        vm((256, 896), F32),
        vm((256, 896), F32),
        vm((256, 896), F32),
        vm((512, 896), BF16),
        vm((4, 8, 128), F32),
        vm((4, 8, 128), F32),
        vm((4, 128, 128), F32),
        vm((512, 128), F32),
        vm((2, 4096), F32),
        vm((1, 128), jnp.int32),
        vm((4, 128, 128), BF16),
        vm((128, 512), F32),
        vm((256, 128), F32),
        vm((3, 8, 256), F32),
        vm((13, 8, 256), F32),
        vm((2, 1, 256), F32),
        vm((256, 128), F32),
        vm((128, 128), F32),
        vm((2, 4, 4, 8, 16, 256), BF16),
        vm((2, 2, 2, 8, 16, 256), BF16),
        vm((2, 2, 2, 8, 16, 256), BF16),
        vm((2, 2, 4, 8, 16, 256), BF16),
        vm((2, 4, 8, 16, 256), BF16),
        vm((2, 3, 8, 16, 256), BF16),
        vm((2, 8, 16, 256), BF16),
        vm((2, 7, 16, 256), BF16),
        vm((4, 1, 256), F32),
        vm((13, 1, 256), F32),
        vm((1, 256), F32),
        vm((2, 16, 256), F32),
        dma((8,)),
        dma((6, 3)), dma((6, 3)),
        dma((2, 4, 3)), dma((2, 4, 3)),
        dma((8, 3)), dma((8, 3)),
        dma((3,)), dma((3,)),
        dma((9,)), dma((9,)),
        dma((2, 3)), dma((2, 3)),
        dma((7,)), dma((7,)),
        dma((2, 5, 3)), dma((2, 5, 3)),
        dma((2, 2, 7)), dma((2, 2, 7)),
        dma((2, 13)),
    ]
    whole = pl.BlockSpec(memory_space=pltpu.HBM)
    vmem = pl.BlockSpec(memory_space=pltpu.VMEM)
    loss, head_grad, hidden_grad, gain_grad = pl.pallas_call(
        kernel,
        name="distill",
        out_shape=(
            vm((1, 128), F32),
            vm((2048, 896), BF16),
            vm((16, 512), BF16),
            vm((1, 16), F32),
        ),
        in_specs=[whole] * 4,
        out_specs=(vmem,) * 4,
        scratch_shapes=scratch,
        cost_estimate=pl.CostEstimate(flops=10**10, bytes_accessed=2 * 10**7, transcendentals=10**6),
        compiler_params=pltpu.CompilerParams(
            collective_id=0, has_side_effects=True, vmem_limit_bytes=59 * 2**20
        ),
    )(hidden_states, output_head_weights, norm_gains, label_ids.reshape(1, 128))
    loss, head_grad, hidden_grad, gain_grad = pl.pallas_call(
        store,
        name="store",
        out_shape=[jax.ShapeDtypeStruct(a.shape, a.dtype) for a in (loss, head_grad, hidden_grad, gain_grad)],
        in_specs=[vmem] * 4,
        out_specs=[pl.BlockSpec(memory_space=pltpu.HBM)] * 4,
        scratch_shapes=[dma((4,))],
        compiler_params=pltpu.CompilerParams(vmem_limit_bytes=4 * 2**20),
    )(loss, head_grad, hidden_grad, gain_grad)
    return loss.reshape(128), head_grad, hidden_grad, gain_grad.reshape(16)


def solution(mesh):
    placed = (P("grp", "seq", None), P("grp", None, ("vocab", "seq")), P(), P("seq"))
    return jax.shard_map(
        per_device,
        mesh=mesh,
        in_specs=placed,
        out_specs=(
            P("seq"),
            P("grp", ("vocab", "seq")),
            P(("grp", "vocab", "seq"), None),
            P(("grp", "vocab", "seq")),
        ),
        check_vma=False,
    )
```

```python
import jax
import jax.numpy as jnp
from jax import lax
from jax.experimental import pallas as pl
from jax.experimental.pallas import tpu as pltpu
from jax.sharding import PartitionSpec as P

SOFTEN_TEMP = 2.0
LABEL_WEIGHT = 0.5
EPSILON = 1e-06
MESH = pl.DeviceIdType.MESH
F32, BF16 = jnp.float32, jnp.bfloat16
NX, NY, NZ = 4, 4, 8
Y_SUB, Z_SUB = 512, 128
Y_PARTS = 4
Y_PART = Y_SUB // Y_PARTS
Z_BASE = NY * Y_SUB
X_BASE = Z_BASE + NZ * Z_SUB
ROWS = 128
PEERS = [(0, 0, d) for d in (1, 2, 3)] + [(0, d, 0) for d in (1, 2, 3)] + [(d, 0, 0) for d in range(1, 8)]


def each(count, body):
    def step(i, carry):
        body(i)
        return carry

    lax.fori_loop(0, count, step, 0)


def kernel(
    hs, w_hbm, gains_hbm, label_hbm,
    loss_out, head_out, hidden_out, gain_out,
    xg, nrm, w, w1h, n1h, n1t, z, zp, e_own, e_given, lg,
    info, info1, invb, labb, gains, label, xblk, ut,
    statc, st_send, st_recv, losses, colb, gainb,
    ng, q1, q2, r1, s2, r2, s3, r3, rt_s, rt_r, rt_other, fin,
    loc, xs_s, xs_r, ys_s, ys_r, zs_s, zs_r, in_s, in_r, pr_s, pr_r,
    sa_s, sa_r, sz_s, sz_r, ab_s, ab_r, cz_s, cz_r, rt_sem,
):
    g = lax.axis_index("grp")
    v = lax.axis_index("vocab")
    s = lax.axis_index("seq")
    zc = lax.div(v, NY)
    yc = lax.rem(v, NY)
    other = 1 - g
    is_teacher = g == 0

    def device(dz, dy, dx):
        return {
            "grp": g,
            "vocab": lax.rem(zc + dz, NZ) * NY + lax.rem(yc + dy, NY),
            "seq": lax.rem(s + dx, NX),
        }

    partner = {"grp": other, "vocab": v, "seq": s}

    def remote(src, dst, ssem, rsem, to):
        return pltpu.make_async_remote_copy(
            src_ref=src, dst_ref=dst, send_sem=ssem, recv_sem=rsem, device_id=to, device_id_type=MESH
        )

    load_x = pltpu.make_async_copy(hs.at[0], xg.at[s], loc.at[0])
    load_g = pltpu.make_async_copy(gains_hbm, gains, loc.at[1])
    load_l = pltpu.make_async_copy(label_hbm, label, loc.at[2])
    load_w = pltpu.make_async_copy(w_hbm.at[0], w, loc.at[3])
    load_x.start()
    load_g.start()
    load_l.start()

    barrier = pltpu.get_barrier_semaphore()
    for dz, dy, dx in PEERS:
        pl.semaphore_signal(barrier, inc=1, device_id=device(dz, dy, dx), device_id_type=MESH)
    pl.semaphore_signal(barrier, inc=1, device_id=partner, device_id_type=MESH)
    pl.semaphore_wait(barrier, len(PEERS) + 1)

    def y_cols(y, part):
        return pl.ds(pl.multiple_of(y * Y_SUB + part * Y_PART, Y_PART), Y_PART)

    def z_cols(at):
        return pl.ds(pl.multiple_of(Z_BASE + at * Z_SUB, 128), Z_SUB)

    def x_copy(kind, d, to):
        cols = y_cols(yc, kind - 1) if kind else z_cols(zc)
        at = s if to else lax.rem(s + NX - d, NX)
        dst = xg.at[at, :, cols]
        return remote(
            dst, dst, xs_s.at[kind, d - 1], xs_r.at[kind, d - 1], device(0, 0, d)
        )

    def x_near(part, k, to):
        d = 1 + 2 * k
        cols = pl.ds(X_BASE + 512 * (k if part == 0 else 1 - k), 512)
        at = s if to else lax.rem(s + NX - d, NX)
        dst = xg.at[at, :, cols]
        return remote(dst, dst, xs_s.at[1 + Y_PARTS + part, k], xs_r.at[1 + Y_PARTS + part, k], device(0, 0, d))

    def x_relay(k, to):
        d = 1 + 2 * k
        ref = xg.at[lax.rem(s + (NX - d if to else 2), NX), :, pl.ds(X_BASE + 512 * k, 512)]
        return remote(ref, ref, xs_s.at[3 + Y_PARTS, k], xs_r.at[3 + Y_PARTS, k], device(0, 0, d))

    def info_copy(d, to):
        at = s if to else lax.rem(s + NX - d, NX)
        return remote(info.at[at], info.at[at], in_s.at[d - 1], in_r.at[d - 1], device(0, 0, d))

    def x_start(kind):
        each(3, lambda i: x_copy(kind, i + 1, True).start())

    load_x.wait()
    for kind in range(1 + Y_PARTS):
        x_start(kind)
    load_w.start()

    half_w = pl.ds(0, 2048)

    def w_copy():
        return remote(w_hbm.at[0, half_w, :], w1h, pr_s.at[0], pr_r.at[0], partner)

    load_w1 = pltpu.make_async_copy(w_hbm.at[0, pl.ds(2048, 2048), :], w1h, loc.at[4])

    @pl.when(g == 1)
    def _():
        w_copy().start()
        load_w1.start()

    load_g.wait()
    load_l.wait()
    total = jnp.zeros((128, 128), F32)
    for b in range(32):
        part = xg[s, :, pl.ds(b * 128, 128)].astype(F32)
        total += part * part
    mean = jnp.sum(total, axis=1, keepdims=True) * (1.0 / 4096)
    inverse = lax.rsqrt(mean + EPSILON)
    inverse_rows = jnp.transpose(jnp.broadcast_to(inverse, (128, 128)))[0:8]
    sub8 = lax.broadcasted_iota(jnp.int32, (8, 128), 0)
    label_rows = jnp.broadcast_to(label[...].astype(F32), (8, 128))
    info[s] = jnp.where(sub8 == 1, label_rows, inverse_rows)

    each(3, lambda i: info_copy(i + 1, True).start())

    def y_copy(part, k, d, to):
        shard = lax.rem(s + NX - d, NX)
        dy = 1 + 2 * k
        ref = xg.at[shard, :, y_cols(yc if to else lax.rem(yc + NY - dy, NY), part)]
        return remote(ref, ref, ys_s.at[part, k, d - 1], ys_r.at[part, k, d - 1], device(0, dy, 0))

    def y_relay(part, k, d, to):
        shard = lax.rem(s + NX - d, NX)
        dy = 1 + 2 * k
        ref = xg.at[shard, pl.ds(64 * k, 64), y_cols(lax.rem(yc + (NY - dy if to else 2), NY), part)]
        return remote(ref, ref, ys_s.at[part, 2 + k, d - 1], ys_r.at[part, 2 + k, d - 1], device(0, dy, 0))

    def z_copy(slot, d, to):
        shard = lax.rem(s + NX - d, NX)
        k = slot % 2
        hops = (2, 1, 1, 2)[slot // 2]
        far = (2, 1, 3, 4)[slot // 2]
        step = NZ - hops if k else hops
        away = far if k else NZ - far
        at = lax.rem(zc + (away + step) % NZ, NZ) if to else lax.rem(zc + away, NZ)
        rows = pl.ds(64 * k, 64) if slot >= 6 else pl.ds(0, 128)
        ref = xg.at[shard, rows, z_cols(at)]
        return remote(ref, ref, zs_s.at[slot, d - 1], zs_r.at[slot, d - 1], device(step, 0, 0))

    def forward_z(i):
        x_copy(0, i + 1, False).wait_recv()
        for slot in range(4):
            z_copy(slot, i + 1, True).start()

    def pass_z(i):
        for k in range(2):
            z_copy(k, i + 1, False).wait_recv()
            z_copy(4 + k, i + 1, True).start()
            z_copy(6 + k, i + 1, True).start()

    def forward_y(part, i):
        x_copy(1 + part, i + 1, False).wait_recv()
        for k in range(2):
            y_copy(part, k, i + 1, True).start()

    def pass_y(part, i):
        for k in range(2):
            y_copy(part, k, i + 1, False).wait_recv()
            y_relay(part, k, i + 1, True).start()

    each(3, forward_z)
    each(3, lambda i: forward_y(0, i))
    for part in range(2):
        for k in range(2):
            x_near(part, k, True).start()
    for part in range(1, Y_PARTS):
        each(3, lambda i, part=part: forward_y(part, i))
    each(3, pass_z)
    for k in range(2):
        x_near(0, k, False).wait_recv()
        x_relay(k, True).start()
    for part in range(Y_PARTS // 2):
        each(3, lambda i, part=part: pass_y(part, i))

    each(3, lambda i: info_copy(i + 1, False).wait_recv())
    tall = jnp.transpose(jnp.concatenate([info[i] for i in range(4)] + [jnp.zeros((96, 128), F32)], axis=0))
    for i in range(4):
        invb[i] = jnp.broadcast_to(tall[:, 8 * i : 8 * i + 1], (128, 128))
        labb[pl.ds(128 * i, 128), :] = jnp.broadcast_to(tall[:, 8 * i + 1 : 8 * i + 2], (128, 128))
    load_w.wait()

    def normalized(f0, width):
        for b in range(width // 128):
            cols = pl.ds(pl.multiple_of(f0 + b * 128, 128), 128)
            gain = jnp.where(is_teacher, gains[0:1, cols], gains[1:2, cols])
            for i in range(4):
                unit = xg[i, :, cols].astype(F32) * invb[i]
                nrm[pl.ds(i * 128, 128), cols] = (unit * gain).astype(BF16)

    def accumulate(f0, width, first=False):
        normalized(f0, width)
        cols = pl.ds(pl.multiple_of(f0, 128), width)
        product = jnp.dot(nrm[:, cols], w[cols, :], preferred_element_type=F32)
        if first:
            z[...] = product
        else:
            z[...] += product

    accumulate(yc * Y_SUB, Y_SUB, first=True)
    for part in range(Y_PARTS // 2, Y_PARTS):
        each(3, lambda i, part=part: pass_y(part, i))

    def add_y(i):
        accumulate(lax.rem(yc + 1 + 2 * i, NY) * Y_SUB, Y_SUB)

    each(2, add_y)

    def take_z(i):
        for slot in range(2, 8):
            z_copy(slot, i + 1, False).wait_recv()

    each(3, take_z)
    accumulate(Z_BASE, 512)
    accumulate(Z_BASE + 512, 512)

    def take_y(i):
        for part in range(Y_PARTS):
            for k in range(2):
                y_relay(part, k, i + 1, False).wait_recv()

    each(3, take_y)
    accumulate(lax.rem(yc + 2, NY) * Y_SUB, Y_SUB)
    for k in range(2):
        x_near(1, k, False).wait_recv()
    x_relay(0, False).wait_recv()
    accumulate(X_BASE, 512)
    x_relay(1, False).wait_recv()

    own = pl.ds(pl.multiple_of(g * 256, 256), 256)
    theirs = pl.ds(pl.multiple_of(other * 256, 256), 256)
    halves = ((0, 512), (512, 384))

    def z_trade(k):
        cols = pl.ds(*halves[k])
        return remote(z.at[theirs, cols], zp.at[:, cols], pr_s.at[(1, 7)[k]], pr_r.at[(1, 7)[k]], partner)

    normalized(X_BASE + 512, 512)
    for k in range(2):
        last = pl.ds(X_BASE + 512, 512)
        cols = pl.ds(*halves[k])
        z[:, cols] += jnp.dot(nrm[:, last], w[last, cols], preferred_element_type=F32)
        z_trade(k).start()

    lane = lax.broadcasted_iota(jnp.int32, (ROWS, 128), 1)
    column = lax.broadcasted_iota(jnp.int32, (ROWS, 896), 1)
    vs = v * NX + s

    def half_rows(r):
        return pl.ds(pl.multiple_of(r * ROWS, ROWS), ROWS)

    def own_rows(r):
        return pl.ds(pl.multiple_of(g * 256 + r * ROWS, ROWS), ROWS)

    def labels_at(r):
        return labb[own_rows(r), 0:1].astype(jnp.int32) - vs * 896

    def own_totals(r):
        rows = half_rows(r)
        mine = z[own_rows(r), :] * (1.0 / SOFTEN_TEMP)
        top = jnp.max(mine, axis=1, keepdims=True)
        e = jnp.exp(mine - top)
        e_own[rows, :] = e
        total = jnp.sum(e, axis=1, keepdims=True)
        statc[rows, :] = jnp.where(lane == 0, top, jnp.broadcast_to(total, (ROWS, 128)))

    each(256 // ROWS, own_totals)
    teacher_block = lax.div(vs, 8)
    block = g * 16 + teacher_block

    def block_cols(b):
        return pl.ds(pl.multiple_of(b * 128, 128), 128)

    xblk_copy = remote(xg.at[:, :, block_cols(teacher_block)], xblk, pr_s.at[2], pr_r.at[2], partner)
    info_pair = remote(info, info1, pr_s.at[3], pr_r.at[3], partner)
    n1_copy = remote(nrm.at[:, half_w], n1h, pr_s.at[4], pr_r.at[4], partner)
    own_block = pltpu.make_async_copy(xg.at[:, :, block_cols(block)], xblk, loc.at[5])
    own_info = pltpu.make_async_copy(info, info1, loc.at[6])
    own_n1 = pltpu.make_async_copy(nrm.at[:, pl.ds(2048, 2048)], n1h, loc.at[7])

    for k in range(2):
        z_trade(k).wait()


    @pl.when(g == 1)
    def _():
        xblk_copy.start()
        info_pair.start()
        n1_copy.start()
        own_block.start()
        own_info.start()
        own_n1.start()

    def totals(r):
        rows = half_rows(r)
        mine = z[own_rows(r), :] * (1.0 / SOFTEN_TEMP)
        given = zp[rows, :] * (1.0 / SOFTEN_TEMP)
        top = jnp.max(given, axis=1, keepdims=True)
        e = jnp.exp(given - top)
        e_given[rows, :] = e
        total = jnp.sum(e, axis=1, keepdims=True)
        e0 = jnp.where(is_teacher, e_own[rows, :], e)
        gap = jnp.where(is_teacher, mine - given, given - mine)
        cross = jnp.sum(e0 * gap, axis=1, keepdims=True)
        z1 = jnp.where(is_teacher, given, mine)
        picked = jnp.sum(jnp.where(column == labels_at(r), z1, 0.0), axis=1, keepdims=True)
        stats = statc[rows, :]
        own_at = jnp.where(is_teacher, 0, 3)
        own_top, own_total = stats[:, 0:1], stats[:, 1:2]
        for i, value in enumerate((own_top, own_total)):
            stats = jnp.where(lane == own_at + i, value, stats)
        for i, value in enumerate((top, total)):
            stats = jnp.where(lane == 3 - own_at + i, value, stats)
        stats = jnp.where(lane == 2, cross, stats)
        statc[rows, :] = jnp.where(lane == 5, picked, stats)

    each(256 // ROWS, totals)
    local = jnp.transpose(statc[...])[0:8]
    st_send[0] = local

    def merge(parts):
        m0 = parts[0][0:1]
        m1 = parts[0][3:4]
        for p in parts[1:]:
            m0 = jnp.maximum(m0, p[0:1])
            m1 = jnp.maximum(m1, p[3:4])
        t0 = cross = t1 = picked = jnp.zeros((1, 256), F32)
        for p in parts:
            s0 = jnp.exp(p[0:1] - m0)
            s1 = jnp.exp(p[3:4] - m1)
            t0 += s0 * p[1:2]
            cross += s0 * p[2:3]
            t1 += s1 * p[4:5]
            picked += p[5:6]
        return jnp.concatenate([m0, t0, cross, m1, t1, picked, picked, picked], axis=0)

    def st_copy(axis, d):
        to = device(0, 0, d) if axis == 0 else device(0, d, 0) if axis == 1 else device(d, 0, 0)
        sems = (sz_s.at[d - 1], sz_r.at[d - 1]) if axis == 2 else (sa_s.at[axis, d - 1], sa_r.at[axis, d - 1])
        return remote(st_send.at[axis], st_recv.at[axis * 3 + d - 1], *sems, to)

    def sent_gather():
        for kind in range(1 + Y_PARTS):
            each(3, lambda i, kind=kind: x_copy(kind, i + 1, True).wait_send())
        for k in range(2):
            for part in range(2):
                x_near(part, k, True).wait_send()
            x_relay(k, True).wait_send()

        def sent_yz(i):
            info_copy(i + 1, True).wait_send()
            for part in range(Y_PARTS):
                for k in range(2):
                    y_copy(part, k, i + 1, True).wait_send()
                    y_relay(part, k, i + 1, True).wait_send()
            for slot in range(8):
                z_copy(slot, i + 1, True).wait_send()

        each(3, sent_yz)

    def prepare():
        @pl.when(g == 0)
        def _():
            n1_copy.wait_recv()
            xblk_copy.wait_recv()
            info_pair.wait_recv()

        @pl.when(g == 1)
        def _():
            own_n1.wait()
            own_block.wait()
            own_info.wait()

        def flip(i):
            cols = pl.ds(pl.multiple_of(i * 128, 128), 128)
            n1t[cols, :] = jnp.transpose(n1h[:, cols])

        each(16, flip)

        for i in range(4):
            unit = jnp.transpose(xblk[i].astype(F32)) * info1[i, 0:1]
            ut[:, pl.ds(i * 128, 128)] = unit
        gain_col = jnp.transpose(jnp.broadcast_to(gains[1:2, block_cols(block)], (128, 128)))
        gainb[...] = gain_col

        @pl.when(g == 0)
        def _():
            w_copy().wait_recv()

        @pl.when(g == 1)
        def _():
            load_w1.wait()

    merged = local
    for axis, count in ((0, 3), (1, 3), (2, 7)):
        if axis:
            st_send[axis] = merged
        each(count, lambda i, axis=axis: st_copy(axis, i + 1).start())
        if axis == 1:
            sent_gather()
        if axis == 2:
            prepare()
        each(count, lambda i, axis=axis: st_copy(axis, i + 1).wait_recv())
        merged = merge([merged] + [st_recv[axis * 3 + i] for i in range(count)])

    lse0 = merged[0:1] + jnp.log(merged[1:2])
    lse1 = merged[3:4] + jnp.log(merged[4:5])
    loss = merged[2:3] / merged[1:2] - lse0 + lse1 + LABEL_WEIGHT * (lse1 - merged[5:6])
    losses[g] = loss
    loss_trade = remote(losses.at[g], losses.at[g], pr_s.at[8], pr_r.at[8], partner)
    scale = 128 * 896 / 16.0 / SOFTEN_TEMP
    a0 = -scale * jnp.exp(local[0:1] - lse0)
    a1 = (scale * (1.0 + LABEL_WEIGHT)) * jnp.exp(local[3:4] - lse1)
    pair = [jnp.where(is_teacher, a0, a1), jnp.where(is_teacher, a1, a0)]
    colb[...] = jnp.transpose(jnp.concatenate(pair + [jnp.zeros((126, 256), F32)], axis=0))

    def gradient(r):
        rows = half_rows(r)
        cols = colb[rows, :]
        target = jnp.where(column == labels_at(r), scale * LABEL_WEIGHT, 0.0)
        lg[own_rows(r), :] = (cols[:, 0:1] * e_own[rows, :] + cols[:, 1:2] * e_given[rows, :] - target).astype(BF16)

    each(256 // ROWS, gradient)
    lg_trade = remote(lg.at[own, :], lg.at[own, :], pr_s.at[5], pr_r.at[5], partner)
    lg_trade.start()
    loss_trade.start()

    def first(h):
        return s + (yc - s) * h

    def second(h):
        return yc + (s - yc) * h

    def a_copy(h, k, part):
        d = 1 + 2 * k
        to = device(0, d * h, d * (1 - h))
        blocks = pl.ds(2 * ((k + part) % 2), 2)
        sems = (ab_s.at[h, k, part], ab_r.at[h, k, part])
        if part == 0:
            return remote(ng.at[h, lax.rem(first(h) + 2, 4), blocks], q1.at[h, k], *sems, to)
        src = ng.at[h, lax.rem(first(h) + d, 4), blocks] if part == 1 else q2.at[h, k]
        return remote(src, r1.at[h, k, blocks], *sems, to)

    def rt_copy(step, d):
        to = (device(d, 0, 0), device(0, 0, d), device(0, d, 0))[step]
        slot = (0, 7, 10)[step] + d - 1
        return remote(rt_s.at[step], rt_r.at[slot], rt_sem.at[0, slot], rt_sem.at[1, slot], to)

    def start_rt(step):
        each((7, 3, 3)[step], lambda i: rt_copy(step, i + 1).start())

    def take_rt(step):
        count, slot = ((7, 0), (3, 7), (3, 10))[step]
        each(count, lambda i: rt_copy(step, i + 1).wait_recv())
        total = rt_s[step]
        for i in range(count):
            total += rt_r[slot + i]
        rt_s[step + 1] = total

    rt_trade = remote(rt_s.at[3], rt_other, pr_s.at[6], pr_r.at[6], partner)

    def b_copy(h, d):
        to = device(0, d * (1 - h), d * h)
        return remote(s2.at[h, lax.rem(second(h) + d, 4)], r2.at[h, d - 1], ab_s.at[h, 3, d - 1], ab_r.at[h, 3, d - 1], to)

    def c_copy(h, d):
        return remote(s3.at[h, lax.rem(zc + d, NZ)], r3.at[h, d - 1], cz_s.at[h, 0, d - 1], cz_r.at[h, 0, d - 1], device(d, 0, 0))

    def states_grad(h):
        tokens = lg[pl.ds(pl.multiple_of(h * 256, 256), 256), :]

        def shard(a):
            rows = []
            for k in range(NZ):
                for b in range(4):
                    at = k * 256 + b * (64 - 48 * h) + a * (16 + 48 * h)
                    rows.append(w1h[pl.ds(pl.multiple_of(at, 16), 16), :])
            rows = jnp.concatenate(rows, axis=0)
            product = lax.dot_general(rows, tokens, (((1,), (1,)), ((), ())), preferred_element_type=F32)
            for k in range(NZ):
                for b in range(4):
                    ng[h, a, b, k] = product[(4 * k + b) * 16 : (4 * k + b) * 16 + 16].astype(BF16)

        shard(lax.rem(first(h) + 2, 4))
        for k in range(2):
            a_copy(h, k, 0).start()
        for k in range(2):
            shard(lax.rem(first(h) + 1 + 2 * k, 4))
            a_copy(h, k, 1).start()
        shard(first(h))

    def pass_a(h):
        for k in range(2):
            a_copy(h, k, 0).wait_recv()
            at = lax.rem(first(h) + 1 + 2 * k, 4)

            def add(i, k=k, at=at):
                for b in range(2):
                    q2[h, k, b, i] = (ng[h, at, 2 * k + b, i].astype(F32) + q1[h, k, b, i].astype(F32)).astype(BF16)

            each(NZ, add)
            a_copy(h, k, 2).start()

    def start_b(h):
        for k in range(2):
            a_copy(h, k, 1).wait_recv()
            a_copy(h, k, 2).wait_recv()
        mine = first(h)

        def add(b):
            for k in range(NZ):
                total = ng[h, mine, b, k].astype(F32)
                for i in range(2):
                    total += r1[h, i, b, k].astype(F32)
                s2[h, b, k] = total.astype(BF16)

        each(4, add)

        def go(i):
            b_copy(h, i + 1).start()

        each(3, go)

    def start_c(h):
        def got(i):
            b_copy(h, i + 1).wait_recv()

        each(3, got)
        mine = second(h)
        for k in range(NZ):
            total = s2[h, mine, k].astype(F32)
            for i in range(3):
                total += r2[h, i, k].astype(F32)
            s3[h, k] = total.astype(BF16)

        def go(i):
            c_copy(h, i + 1).start()

        each(7, go)

    def finish(h):
        def got(i):
            c_copy(h, i + 1).wait_recv()

        each(7, got)
        total = s3[h, zc].astype(F32)
        for i in range(7):
            total += r3[h, i].astype(F32)
        fin[h] = total

    states_grad(g)
    lg_trade.wait_recv()
    states_grad(other)

    def along(r):
        rows = pl.ds(pl.multiple_of(r * ROWS, ROWS), ROWS)
        grad = lg[pl.ds(pl.multiple_of(g * 256 + r * ROWS, ROWS), ROWS), :].astype(F32)
        z1 = jnp.where(is_teacher, zp[rows, :], z[pl.ds(pl.multiple_of(g * 256 + r * ROWS, ROWS), ROWS), :])
        total = jnp.sum(grad * z1, axis=1, keepdims=True) * (1.0 / SOFTEN_TEMP)
        statc[rows, :] = jnp.broadcast_to(total, (ROWS, 128))

    each(256 // ROWS, along)
    rt_s[0] = jnp.transpose(statc[...])[0:1]
    start_rt(0)
    lg_trade.wait_send()
    loss_trade.wait()

    def head_tile(i):
        rows = pl.ds(pl.multiple_of(i * 512, 512), 512)
        head_out[rows, :] = jnp.dot(n1t[rows, :], lg[...], preferred_element_type=F32).astype(BF16)

    each(2, head_tile)
    pass_a(g)
    head_tile(2)
    pass_a(other)
    head_tile(3)
    for axis, count in ((0, 3), (1, 3), (2, 7)):
        each(count, lambda i, axis=axis: st_copy(axis, i + 1).wait_send())
    @pl.when(g == 1)
    def _():
        w_copy().wait_send()
        xblk_copy.wait_send()
        info_pair.wait_send()
        n1_copy.wait_send()

    start_b(g)
    start_b(other)

    def sent_a(h):
        for part in range(3):
            for k in range(2):
                a_copy(h, k, part).wait_send()

    each(2, sent_a)
    take_rt(0)
    start_rt(1)
    start_c(g)
    start_c(other)
    each(2, lambda h: each(3, lambda i: b_copy(h, i + 1).wait_send()))
    each(7, lambda i: rt_copy(0, i + 1).wait_send())
    take_rt(1)
    start_rt(2)
    take_rt(2)
    rt_trade.start()
    finish(g)
    finish(other)
    rt_trade.wait_recv()

    inv_row = jnp.concatenate([info1[i, 0:1] for i in range(4)], axis=1)
    mine16 = pl.ds(pl.multiple_of(lax.rem(vs, 8) * 16, 16), 16)
    gain16 = gainb[mine16, 0:1]
    gain_total = jnp.zeros((16, 1), F32)
    for h in range(2):
        cols = pl.ds(h * 256, 256)
        unit = ut[mine16, cols]
        grad = fin[h]
        row_mean = jnp.where(g == h, rt_s[3], rt_other[...]) * (SOFTEN_TEMP / 4096)
        hidden = inv_row[:, h * 256 : h * 256 + 256] * (grad * gain16 - unit * row_mean)
        hidden_out[:, cols] = hidden.astype(BF16)
        gain_total += jnp.sum(grad * unit, axis=1, keepdims=True)
    wide = jnp.concatenate([jnp.broadcast_to(gain_total, (16, 128)), jnp.zeros((112, 128), F32)], axis=0)
    gain_out[...] = jnp.transpose(wide)[0:1, 0:16]
    loss_out[...] = losses[lax.div(s, 2), :, pl.ds(pl.multiple_of(lax.rem(s, 2) * 128, 128), 128)]

    each(2, lambda h: each(7, lambda i: c_copy(h, i + 1).wait_send()))
    for step in (1, 2):
        each(3, lambda i, step=step: rt_copy(step, i + 1).wait_send())
    rt_trade.wait_send()

def store(loss, head, hidden, gain, loss_out, head_out, hidden_out, gain_out, sems):
    pairs = ((head, head_out), (hidden, hidden_out), (loss, loss_out), (gain, gain_out))
    copies = [pltpu.make_async_copy(a, b, sems.at[i]) for i, (a, b) in enumerate(pairs)]
    for copy in copies:
        copy.start()
    for copy in copies:
        copy.wait()


def per_device(hidden_states, output_head_weights, norm_gains, label_ids):
    dma = pltpu.SemaphoreType.DMA
    vm = pltpu.VMEM
    scratch = [
        vm((4, 128, 4096), BF16),
        vm((512, 4096), BF16),
        vm((4096, 896), BF16),
        vm((2048, 896), BF16),
        vm((512, 2048), BF16),
        vm((2048, 512), BF16),
        vm((512, 896), F32),
        vm((256, 896), F32),
        vm((256, 896), F32),
        vm((256, 896), F32),
        vm((512, 896), BF16),
        vm((4, 8, 128), F32),
        vm((4, 8, 128), F32),
        vm((4, 128, 128), F32),
        vm((512, 128), F32),
        vm((2, 4096), F32),
        vm((1, 128), jnp.int32),
        vm((4, 128, 128), BF16),
        vm((128, 512), F32),
        vm((256, 128), F32),
        vm((3, 8, 256), F32),
        vm((13, 8, 256), F32),
        vm((2, 1, 256), F32),
        vm((256, 128), F32),
        vm((128, 128), F32),
        vm((2, 4, 4, 8, 16, 256), BF16),
        vm((2, 2, 2, 8, 16, 256), BF16),
        vm((2, 2, 2, 8, 16, 256), BF16),
        vm((2, 2, 4, 8, 16, 256), BF16),
        vm((2, 4, 8, 16, 256), BF16),
        vm((2, 3, 8, 16, 256), BF16),
        vm((2, 8, 16, 256), BF16),
        vm((2, 7, 16, 256), BF16),
        vm((4, 1, 256), F32),
        vm((13, 1, 256), F32),
        vm((1, 256), F32),
        vm((2, 16, 256), F32),
        dma((8,)),
        dma((4 + Y_PARTS, 3)), dma((4 + Y_PARTS, 3)),
        dma((Y_PARTS, 4, 3)), dma((Y_PARTS, 4, 3)),
        dma((8, 3)), dma((8, 3)),
        dma((3,)), dma((3,)),
        dma((9,)), dma((9,)),
        dma((2, 3)), dma((2, 3)),
        dma((7,)), dma((7,)),
        dma((2, 5, 3)), dma((2, 5, 3)),
        dma((2, 2, 7)), dma((2, 2, 7)),
        dma((2, 13)),
    ]
    whole = pl.BlockSpec(memory_space=pltpu.HBM)
    vmem = pl.BlockSpec(memory_space=pltpu.VMEM)
    loss, head_grad, hidden_grad, gain_grad = pl.pallas_call(
        kernel,
        name="distill",
        out_shape=(
            vm((1, 128), F32),
            vm((2048, 896), BF16),
            vm((16, 512), BF16),
            vm((1, 16), F32),
        ),
        in_specs=[whole] * 4,
        out_specs=(vmem,) * 4,
        scratch_shapes=scratch,
        cost_estimate=pl.CostEstimate(flops=10**10, bytes_accessed=2 * 10**7, transcendentals=10**6),
        compiler_params=pltpu.CompilerParams(
            collective_id=0, has_side_effects=True, vmem_limit_bytes=59 * 2**20
        ),
    )(hidden_states, output_head_weights, norm_gains, label_ids.reshape(1, 128))
    loss, head_grad, hidden_grad, gain_grad = pl.pallas_call(
        store,
        name="store",
        out_shape=[jax.ShapeDtypeStruct(a.shape, a.dtype) for a in (loss, head_grad, hidden_grad, gain_grad)],
        in_specs=[vmem] * 4,
        out_specs=[pl.BlockSpec(memory_space=pltpu.HBM)] * 4,
        scratch_shapes=[dma((4,))],
        compiler_params=pltpu.CompilerParams(vmem_limit_bytes=4 * 2**20),
    )(loss, head_grad, hidden_grad, gain_grad)
    return loss.reshape(128), head_grad, hidden_grad, gain_grad.reshape(16)


def solution(mesh):
    placed = (P("grp", "seq", None), P("grp", None, ("vocab", "seq")), P(), P("seq"))
    return jax.shard_map(
        per_device,
        mesh=mesh,
        in_specs=placed,
        out_specs=(
            P("seq"),
            P("grp", ("vocab", "seq")),
            P(("grp", "vocab", "seq"), None),
            P(("grp", "vocab", "seq")),
        ),
        check_vma=False,
    )
```
